512 devices in a mesh: ra: 128 (over z_hi, x, y), slab: 4 (over z_lo, core).
Axes of the slice: x: 4, y: 8, z: 8 (z_hi: 4, z_lo: 2; z = z_hi * 2 + z_lo), core: 2. Of those that a mesh axis runs over, the one named last changes fastest.
Arguments:
- images: bfloat16 [512, 256, 1024], P('ra', 'slab'), may hold values from -6 to 6
- row_taps: bfloat16 [20, 41], replicated, may hold values from -1 to 1
- col_taps: bfloat16 [20, 41], replicated, may hold values from -1 to 1
- coef: float32 [512, 4, 20], replicated, may hold values from -1.25 to 1.25
- blocks: int32 [512, 8], replicated, may hold values from 0 to 3
- boxes: int32 [512, 2], replicated, may hold values from 0 to 8, as said below
- ivar: float32 [512], replicated, may hold values from 0.25 to 4
- counts: int32 [128], replicated, may hold values from 1 to 4, as said below
Outputs:
- coadd: float32 [256, 65536], P('slab', 'ra')
The draws below stay inside these ranges and needn't reach their ends.
Inputs may be any that keep to these rules, and one draw needn't show every extreme that they name: boxes[v, 0] lies below 4 and boxes[v, 1] above it, so every piece crosses from its home patch into the next; both ends are reached. Slots 0 to counts[p] - 1 of home patch p are live; some patch holds 4.
All inputs are finite; a program needn't handle non-finite values.
Results may differ from the reference program's by a relative error of at most 0.0029.
Values may be sent and summed in bfloat16 or wider, within the bound.
A program may use at most 64 MiB of HBM per device.

```python
import math
import jax
import jax.numpy as jnp
from jax import lax

NB = 20
TAPS = 41
NSET = 4
VIS_DEV = 4
C = 512
PATCHES = 128
ROWS = 256
VISITS = 512
SPAN = 1024
TILES = 8


def draw_boxes(key, part):
    key = jax.random.fold_in(key, 11)
    first_key, last_key, pick_key = jax.random.split(key, 3)
    half_tiles = C // 128
    lower = jax.random.randint(first_key, (VISITS,), 0, half_tiles)
    upper = jax.random.randint(last_key, (VISITS,), half_tiles + 1, 2 * half_tiles + 1)
    chosen = jnp.arange(VISITS) == jax.random.randint(pick_key, (), 0, VISITS)
    lower = jnp.where(chosen, 0, lower)
    upper = jnp.where(chosen, 2 * half_tiles, upper)
    return jnp.stack([lower, upper], axis=1).astype(jnp.int32)


def draw_counts(key, part):
    key = jax.random.fold_in(key, 23)
    extra_key, heavy_key, pick_key = jax.random.split(key, 3)
    extra = jax.random.randint(extra_key, (PATCHES,), 0, VIS_DEV)
    heavy = jax.random.randint(heavy_key, (PATCHES,), 0, 4) == 0
    live = 1 + jnp.where(heavy, extra, 0)
    chosen = jnp.arange(PATCHES) == jax.random.randint(pick_key, (), 0, PATCHES)
    return jnp.where(chosen, VIS_DEV, live).astype(jnp.int32)


def set_ends(drawn, stream_key, low, largest):
    index_at = [jax.random.randint(jax.random.fold_in(stream_key, axis), (), 0, length) for axis, length in enumerate(drawn.shape)]
    longest = drawn.shape.index(max(drawn.shape))
    beside = index_at[:longest] + [(index_at[longest] + 1) % drawn.shape[longest]] + index_at[longest + 1:]
    return drawn.at[tuple(index_at)].set(low).at[tuple(beside)].set(largest)


def block_scale(rng, shape, pieces, low, top_value):
    def one(axis_at, parts):
        draws = jax.random.uniform(jax.random.fold_in(jax.random.fold_in(rng, 6), axis_at), (parts,), jnp.float32, low / len(pieces), top_value / len(pieces))
        return jnp.repeat(jnp.exp(draws), shape[axis_at] // parts).reshape((-1,) + (1,) * (len(shape) - axis_at - 1))

    gain = one(*pieces[0])
    for cut in pieces[1:]:
        gain = gain * one(*cut)
    return gain


def normal_values(key, extent, deviation, most, pieces=(), kind=jnp.bfloat16):
    values = jax.random.normal(key, extent, jnp.float32) * deviation
    if len(pieces) > 0:
        values = block_scale(key, extent, pieces, -0.22, 0.18) * values
    return jnp.clip(values, min=-most, max=most).astype(kind)


def setup_inputs(seed: int = 0) -> dict:
    key_list = jax.random.split(jax.random.key(seed), 9)
    images = normal_values(key_list[0], (VISITS, ROWS, SPAN), 1.0, 6.0, ((0, 128), (1, 4)))
    row_taps = normal_values(key_list[1], (NB, TAPS), TAPS ** -0.5, 1.0)
    col_taps = normal_values(key_list[2], (NB, TAPS), TAPS ** -0.5, 1.0)
    coef = normal_values(key_list[3], (VISITS, NSET, NB), NB ** -0.5, 1.25, (), jnp.float32)
    blocks = set_ends(jax.random.randint(key_list[4], (VISITS, TILES), 0, NSET), jax.random.fold_in(key_list[4], 1), 0, NSET - 1).astype(jnp.int32)
    boxes = draw_boxes(jax.random.fold_in(key_list[8], 71), 0)
    ivar = jnp.clip(jnp.exp(jax.random.uniform(key_list[6], (VISITS,), jnp.float32, math.log(0.25), math.log(4.0))), 0.25, 4.0)
    counts = draw_counts(jax.random.fold_in(key_list[8], 71), 0)
    return {"images": images, "row_taps": row_taps, "col_taps": col_taps, "coef": coef, "blocks": blocks, "boxes": boxes, "ivar": ivar, "counts": counts}


def row_matrix(row_taps, rows):
    taps = row_taps.shape[1]
    reach = taps // 2
    offsets = jnp.arange(rows + 2 * reach)[None, :] - jnp.arange(rows)[:, None]
    onehot = (offsets[:, :, None] == jnp.arange(taps)[None, None, :]).astype(jnp.float32)
    return jnp.einsum('bk,rjk->brj', row_taps.astype(jnp.float32), onehot,
                      precision=lax.Precision.HIGHEST).astype(jnp.bfloat16)


def col_matrix(col_taps):
    basis, taps = col_taps.shape
    reach = taps // 2
    offsets = jnp.arange(384)[:, None] - 128 - jnp.arange(128)[None, :] + reach
    onehot = (offsets[:, :, None] == jnp.arange(taps)[None, None, :]).astype(jnp.float32)
    full = jnp.einsum('bk,jck->bjc', col_taps.astype(jnp.float32), onehot,
                      precision=lax.Precision.HIGHEST).astype(jnp.bfloat16)
    return full.reshape(basis, 3, 128, 128)


def convolve(row_mat, col_mat, piece, first, count_tiles, tile_coef):
    basis, rows, _ = row_mat.shape
    width = piece.shape[1]
    smooth = jnp.dot(row_mat.reshape(basis * rows, -1), piece, preferred_element_type=jnp.float32)
    smooth = lax.optimization_barrier(smooth.astype(jnp.bfloat16)).astype(jnp.float32)
    smooth = smooth.reshape(basis, rows, width // 128, 128)
    smooth = jnp.pad(smooth, ((0, 0), (0, 0), (1, 1), (0, 0)))
    total = jnp.zeros((basis, rows, count_tiles, 128), jnp.float32)
    for shift_tile in range(3):
        total = total + jnp.einsum('brtk,bkc->brtc', smooth[:, :, first + shift_tile:first + shift_tile + count_tiles],
                                   col_mat[:, shift_tile].astype(jnp.float32), precision=lax.Precision.HIGHEST)
    result = jnp.sum(total * tile_coef[:, None, :, None], axis=0)
    return result.reshape(rows, count_tiles * 128)


def reference(images, row_taps, col_taps, coef, blocks, boxes, ivar, counts):
    visits, rows, span = images.shape
    half = span // 2
    tiles = span // 128
    reach = row_taps.shape[1] // 2
    row_mat = row_matrix(row_taps, rows)
    col_mat = col_matrix(col_taps)
    columns = jnp.arange(span).astype(jnp.int32)
    sets = coef.shape[1]

    def accumulate(index, carry):
        numer, denom = carry
        visit = jnp.asarray(index).astype(jnp.int32)
        home = visit // VIS_DEV
        live = (visit % VIS_DEV) < counts[home]
        inside = (columns >= boxes[visit, 0] * 128) & (columns < boxes[visit, 1] * 128)
        piece = jnp.where(inside[None, :], images[visit], jnp.zeros((), images.dtype))
        piece = jnp.pad(piece, ((reach, reach), (0, 0)))
        picks = (blocks[visit][None, :] == jnp.arange(sets)[:, None]).astype(jnp.float32)
        tile_coef = jnp.sum(coef[visit][:, :, None] * picks[:, None, :], axis=0)
        conv = convolve(row_mat, col_mat, piece, 0, tiles, tile_coef)
        weight = jnp.where(live & inside, ivar[visit], jnp.zeros((), ivar.dtype))
        start = (home * half).astype(jnp.int32)
        zero = jnp.zeros((), jnp.int32)
        block_now = lax.dynamic_slice(numer, (zero, start), (rows, span))
        numer = lax.dynamic_update_slice(numer, block_now + conv * weight[None, :], (zero, start))
        den_now = lax.dynamic_slice(denom, (start,), (span,))
        denom = lax.dynamic_update_slice(denom, den_now + weight, (start,))
        return numer, denom

    numer = jnp.zeros((rows, (PATCHES + 1) * half), jnp.float32)
    denom = jnp.zeros(((PATCHES + 1) * half,), jnp.float32)
    numer, denom = lax.fori_loop(0, visits, accumulate, (numer, denom))
    wrapped = numer[:, :PATCHES * half].at[:, :half].add(numer[:, PATCHES * half:])
    wrapped_den = denom[:PATCHES * half].at[:half].add(denom[PATCHES * half:])
    return wrapped / jnp.maximum(wrapped_den, 1.0)[None, :]
```

```python
import functools

import jax
import jax.numpy as jnp
from jax import lax
from jax.experimental import pallas as pl
from jax.experimental.pallas import tpu as pltpu
from jax.sharding import PartitionSpec as P

MESH = pl.DeviceIdType.MESH
NB = 20
TAPS = 41
SETS = 4
REACH = 20
SLOTS = 4
ROWS = 64
HALO = 32
DEPTH = ROWS + 2 * HALO
TILE = 128
TILES = 8
HALF = 4
SPAN = TILES * TILE
F32 = jnp.float32
BF16 = jnp.bfloat16


def kernel(npatch, nslab, images, row_taps, col_taps, coef, blocks, boxes, ivar, counts,
           out, piece, coef_v, block_v, row_mat, col_mat, centre, beside, lhs, side, far_out, far_in,
           local_sem, halo_send, halo_recv, far_send, far_recv):
    patch = lax.axis_index("ra")
    slab = lax.axis_index("slab")
    after = lax.rem(patch + 1, npatch)
    before = lax.rem(patch + npatch - 1, npatch)
    has_up = slab > 0
    has_down = slab < nslab - 1

    barrier = pltpu.get_barrier_semaphore()
    pl.semaphore_signal(barrier, inc=1, device_id=(before, slab), device_id_type=MESH)

    @pl.when(has_up)
    def _():
        pl.semaphore_signal(barrier, inc=1, device_id=(patch, slab - 1), device_id_type=MESH)

    @pl.when(has_down)
    def _():
        pl.semaphore_signal(barrier, inc=1, device_id=(patch, slab + 1), device_id_type=MESH)

    lane_block = pl.ds(pl.multiple_of((patch * SLOTS // TILE) * TILE, TILE), TILE)
    local = [
        pltpu.make_async_copy(images, piece.at[:, pl.ds(HALO, ROWS), :], local_sem.at[0]),
        pltpu.make_async_copy(coef.at[:, :, lane_block], coef_v, local_sem.at[1]),
        pltpu.make_async_copy(blocks.at[:, lane_block], block_v, local_sem.at[2]),
    ]
    for copy in local:
        copy.start()

    spans = [pl.ds(3 * TILE, 5 * TILE), pl.ds(0, 3 * TILE)]

    def down(i):
        return pltpu.make_async_remote_copy(
            src_ref=images.at[:, pl.ds(ROWS - HALO, HALO), spans[i]],
            dst_ref=piece.at[:, pl.ds(0, HALO), spans[i]],
            send_sem=halo_send.at[i], recv_sem=halo_recv.at[i],
            device_id=(patch, slab + 1), device_id_type=MESH)

    def up(i):
        return pltpu.make_async_remote_copy(
            src_ref=images.at[:, pl.ds(0, HALO), spans[i]],
            dst_ref=piece.at[:, pl.ds(HALO + ROWS, HALO), spans[i]],
            send_sem=halo_send.at[2 + i], recv_sem=halo_recv.at[2 + i],
            device_id=(patch, slab - 1), device_id_type=MESH)

    tap = lax.broadcasted_iota(jnp.int32, (TAPS, TILE), 0)
    lane = lax.broadcasted_iota(jnp.int32, (TAPS, TILE), 1)
    row_base = jnp.dot(row_taps[...], (lane == tap + (HALO - REACH)).astype(F32).astype(BF16),
                       preferred_element_type=F32)
    for b in range(NB):
        band = jnp.broadcast_to(row_base[b:b + 1, :], (ROWS, TILE))
        band = pltpu.roll(band, 0, 1, stride=1, stride_axis=0)
        row_mat[b * ROWS:(b + 1) * ROWS, :] = band.astype(BF16)

    pl.semaphore_wait(barrier, 1 + has_up.astype(jnp.int32) + has_down.astype(jnp.int32))

    for i in range(2):
        @pl.when(has_down)
        def _():
            down(i).start()

        @pl.when(has_up)
        def _():
            up(i).start()

    @pl.when(jnp.logical_not(has_up))
    def _():
        piece[:, 0:HALO, :] = jnp.zeros((SLOTS, HALO, SPAN), BF16)

    @pl.when(jnp.logical_not(has_down))
    def _():
        piece[:, HALO + ROWS:, :] = jnp.zeros((SLOTS, HALO, SPAN), BF16)

    turned = lax.rem(REACH - tap + TILE, TILE)
    col_base = jnp.dot(col_taps[...], (lane == turned).astype(F32).astype(BF16),
                       preferred_element_type=F32)
    row_at = lax.broadcasted_iota(jnp.int32, (TILE, TILE), 0)
    col_at = lax.broadcasted_iota(jnp.int32, (TILE, TILE), 1)
    near = jnp.abs(row_at - col_at) <= REACH
    for b in range(NB):
        band = jnp.broadcast_to(col_base[b:b + 1, :], (TILE, TILE))
        band = pltpu.roll(band, 0, 1, stride=1, stride_axis=0)
        col_mat[b * TILE:(b + 1) * TILE, :] = jnp.where(near, band, 0.0).astype(BF16)
        col_mat[(NB + b) * TILE:(NB + b + 1) * TILE, :] = jnp.where(near, 0.0, band).astype(BF16)

    local[1].wait()
    local[2].wait()
    turn = lax.rem(TILE - lax.rem(patch * SLOTS, TILE), TILE)
    sets = [pltpu.roll(coef_v[:, s, :], turn, 1) for s in range(SETS)]
    block = pltpu.roll(block_v[...], turn, 1)
    low_lanes = lax.broadcasted_iota(jnp.int32, (NB, TILE), 1) < TILE // 2

    def visit_scalars(home, v):
        visit = home * SLOTS + v
        scale = jnp.where(v < counts[home], ivar[visit], 0.0)
        inside = [jnp.where((t >= boxes[0, visit]) & (t < boxes[1, visit]), 1.0, 0.0) for t in range(TILES)]
        return scale, inside

    own = [visit_scalars(patch, v) for v in range(SLOTS)]
    other = [visit_scalars(before, v) for v in range(SLOTS)]
    chosen = []
    for t in range(TILES):
        pick = block[t:t + 1, :]
        total = jnp.zeros((NB, TILE), F32)
        for s in range(SETS):
            total = total + jnp.where(pick == s, sets[s], 0.0)
        chosen.append(total)
    for v in range(SLOTS):
        scale, inside = own[v]
        spread = [jnp.broadcast_to(chosen[t][:, v:v + 1], (NB, TILE)) * (scale * inside[t]) for t in range(TILES)]
        zero = jnp.zeros((NB, TILE), F32)
        for t in range(TILES):
            left = spread[t - 1] if t > 0 else zero
            right = spread[t + 1] if t + 1 < TILES else zero
            centre[t, v, 0:NB, :] = spread[t]
            beside[t, v, 0:NB, :] = jnp.where(low_lanes, left, right) * inside[t]

    def smooth(u):
        columns = pl.ds(pl.multiple_of(u * TILE, TILE), TILE)
        chunk = 256
        each = chunk // ROWS
        for at in range(NB * ROWS // chunk):
            mid, off = [None] * each, [None] * each
            for pair in range(SLOTS // 2):
                both = jnp.concatenate([piece[2 * pair, :, columns], piece[2 * pair + 1, :, columns]], axis=1)
                part = jnp.dot(row_mat[at * chunk:(at + 1) * chunk, :], both, preferred_element_type=F32)
                for w in range(2):
                    v = 2 * pair + w
                    for j in range(each):
                        b = at * each + j
                        term = part[j * ROWS:(j + 1) * ROWS, w * TILE:(w + 1) * TILE]
                        one = term * centre[u, v, b:b + 1, :]
                        two = term * beside[u, v, b:b + 1, :]
                        mid[j] = one if mid[j] is None else mid[j] + one
                        off[j] = two if off[j] is None else off[j] + two
            for j in range(each):
                b = at * each + j
                lhs[u, :, b * TILE:(b + 1) * TILE] = mid[j].astype(BF16)
                side[u + 1, :, b * TILE:(b + 1) * TILE] = off[j].astype(BF16)

    low = lax.rem(lax.broadcasted_iota(jnp.int32, (ROWS, NB * TILE), 1), TILE) < TILE // 2

    def columns_of(first):
        for t in range(first, first + HALF):
            lhs[t, :, NB * TILE:] = jnp.where(low, side[t + 2], side[t])
        block_lhs = lhs[first:first + HALF].reshape(HALF * ROWS, 2 * NB * TILE)
        return jnp.dot(block_lhs, col_mat[...], preferred_element_type=F32)

    side[0] = jnp.zeros((ROWS, NB * TILE), BF16)
    side[TILES + 1] = jnp.zeros((ROWS, NB * TILE), BF16)
    local[0].wait()

    def halo_wait(i):
        @pl.when(has_up)
        def _():
            down(i).wait_recv()

        @pl.when(has_down)
        def _():
            up(i).wait_recv()

    halo_wait(0)
    lax.fori_loop(0, 5, lambda i, c: (smooth(7 - i), c)[1], 0)
    far = columns_of(HALF)
    for t in range(HALF):
        far_out[:, t * TILE:(t + 1) * TILE] = far[t * ROWS:(t + 1) * ROWS]
    far_copy = pltpu.make_async_remote_copy(
        src_ref=far_out, dst_ref=far_in, send_sem=far_send, recv_sem=far_recv,
        device_id=(after, slab), device_id_type=MESH)
    far_copy.start()

    halo_wait(1)
    lax.fori_loop(0, 3, lambda i, c: (smooth(2 - i), c)[1], 0)
    near_part = columns_of(0)
    far_copy.wait_recv()
    for t in range(HALF):
        weight = jnp.float32(0.0)
        for v in range(SLOTS):
            weight = weight + own[v][0] * own[v][1][t] + other[v][0] * other[v][1][t + HALF]
        total = near_part[t * ROWS:(t + 1) * ROWS] + far_in[:, t * TILE:(t + 1) * TILE]
        out[:, t * TILE:(t + 1) * TILE] = total / jnp.full((ROWS, TILE), jnp.maximum(weight, 1.0), F32)

    far_copy.wait_send()
    for i in range(2):
        @pl.when(has_down)
        def _():
            down(i).wait_send()

        @pl.when(has_up)
        def _():
            up(i).wait_send()


def local_part(npatch, nslab, images, row_taps, col_taps, coef, blocks, boxes, ivar, counts):
    vmem = pl.BlockSpec(memory_space=pltpu.VMEM)
    smem = pl.BlockSpec(memory_space=pltpu.SMEM)
    anyplace = pl.BlockSpec(memory_space=pl.ANY)
    dma = pltpu.SemaphoreType.DMA
    return pl.pallas_call(
        functools.partial(kernel, npatch, nslab),
        out_shape=jax.ShapeDtypeStruct((ROWS, HALF * TILE), F32),
        in_specs=[anyplace, vmem, vmem, anyplace, anyplace, smem, smem, smem],
        out_specs=vmem,
        scratch_shapes=[
            pltpu.VMEM((SLOTS, DEPTH, SPAN), BF16),
            pltpu.VMEM((NB, SETS, TILE), F32),
            pltpu.VMEM((TILES, TILE), jnp.int32),
            pltpu.VMEM((NB * ROWS, DEPTH), BF16),
            pltpu.VMEM((2 * NB * TILE, TILE), BF16),
            pltpu.VMEM((TILES, SLOTS, 24, TILE), F32),
            pltpu.VMEM((TILES, SLOTS, 24, TILE), F32),
            pltpu.VMEM((TILES, ROWS, 2 * NB * TILE), BF16),
            pltpu.VMEM((TILES + 2, ROWS, NB * TILE), BF16),
            pltpu.VMEM((ROWS, HALF * TILE), F32),
            pltpu.VMEM((ROWS, HALF * TILE), F32),
            dma((3,)), dma((4,)), dma((4,)), dma, dma,
        ],
        compiler_params=pltpu.CompilerParams(
            collective_id=0, has_side_effects=True, vmem_limit_bytes=56 << 20),
        cost_estimate=pl.CostEstimate(flops=4_000_000_000, bytes_accessed=2_000_000, transcendentals=0),
    )(images, row_taps, col_taps, coef.transpose(2, 1, 0), blocks.T, boxes.T, ivar, counts)


def solution(mesh):
    return jax.shard_map(
        functools.partial(local_part, mesh.shape["ra"], mesh.shape["slab"]),
        mesh=mesh,
        in_specs=(P("ra", "slab", None), P(), P(), P(), P(), P(), P(), P()),
        out_specs=P("slab", "ra"),
        check_vma=False,
    )
```

```python
import functools

import jax
import jax.numpy as jnp
from jax import lax
from jax.experimental import pallas as pl
from jax.experimental.pallas import tpu as pltpu
from jax.sharding import PartitionSpec as P

MESH = pl.DeviceIdType.MESH
NB = 20
TAPS = 41
SETS = 4
REACH = 20
SLOTS = 4
ROWS = 64
HALO = 32
DEPTH = ROWS + 2 * HALO
PACK = SLOTS * REACH
TILE = 128
TILES = 8
HALF = 4
SPAN = TILES * TILE
F32 = jnp.float32
BF16 = jnp.bfloat16


def kernel(npatch, nslab, images, row_taps, col_taps, coef, blocks, boxes, ivar, counts,
           out, own_rows, packed, above, below, coef_v, block_v, row_mat, col_mat, centre, beside, lhs, side, far_out, far_in,
           local_sem, halo_send, halo_recv, far_send, far_recv):
    patch = lax.axis_index("ra")
    slab = lax.axis_index("slab")
    after = lax.rem(patch + 1, npatch)
    before = lax.rem(patch + npatch - 1, npatch)
    has_up = slab > 0
    has_down = slab < nslab - 1

    barrier = pltpu.get_barrier_semaphore()
    pl.semaphore_signal(barrier, inc=1, device_id=(before, slab), device_id_type=MESH)

    @pl.when(has_up)
    def _():
        pl.semaphore_signal(barrier, inc=1, device_id=(patch, slab - 1), device_id_type=MESH)

    @pl.when(has_down)
    def _():
        pl.semaphore_signal(barrier, inc=1, device_id=(patch, slab + 1), device_id_type=MESH)

    lane_block = pl.ds(pl.multiple_of((patch * SLOTS // TILE) * TILE, TILE), TILE)
    local = [
        pltpu.make_async_copy(images, own_rows, local_sem.at[0]),
        pltpu.make_async_copy(coef.at[:, :, lane_block], coef_v, local_sem.at[1]),
        pltpu.make_async_copy(blocks.at[:, lane_block], block_v, local_sem.at[2]),
    ]
    for copy in local:
        copy.start()

    spans = [pl.ds(5 * TILE, 3 * TILE), pl.ds(3 * TILE, 2 * TILE), pl.ds(0, 3 * TILE)]

    def down(i):
        return pltpu.make_async_remote_copy(
            src_ref=packed.at[pl.ds(PACK, PACK), spans[i]], dst_ref=above.at[:, spans[i]],
            send_sem=halo_send.at[i], recv_sem=halo_recv.at[i],
            device_id=(patch, slab + 1), device_id_type=MESH)

    def up(i):
        return pltpu.make_async_remote_copy(
            src_ref=packed.at[pl.ds(0, PACK), spans[i]], dst_ref=below.at[:, spans[i]],
            send_sem=halo_send.at[3 + i], recv_sem=halo_recv.at[3 + i],
            device_id=(patch, slab - 1), device_id_type=MESH)

    tap = lax.broadcasted_iota(jnp.int32, (TAPS, TILE), 0)
    lane = lax.broadcasted_iota(jnp.int32, (TAPS, TILE), 1)

    def laid(taps, at):
        return jnp.dot(taps[...], (lane == at).astype(F32).astype(BF16), preferred_element_type=F32)

    def rolled(base, b, count):
        band = jnp.broadcast_to(base[b:b + 1, :], (count, TILE))
        return pltpu.roll(band, 0, 1, stride=1, stride_axis=0)

    own_base = laid(row_taps, tap + (HALO - REACH))
    edge_bases = [laid(row_taps, jnp.where(tap < REACH, tap + 4 * v,
                                           jnp.where(tap > REACH, tap + (HALO - REACH) + 4 * v, -1)))
                  for v in range(SLOTS)]
    at_lane = lax.broadcasted_iota(jnp.int32, (ROWS, TILE), 1)
    is_own = (at_lane >= HALO) & (at_lane < HALO + ROWS)
    edges = [((at_lane >= 4 * v) & (at_lane < 4 * v + REACH))
             | ((at_lane >= HALO + ROWS + 4 * v) & (at_lane < HALO + ROWS + 4 * v + REACH)) for v in range(SLOTS)]
    for b in range(NB):
        band = rolled(own_base, b, ROWS)
        for v in range(SLOTS):
            edge = jnp.where(edges[v], rolled(edge_bases[v], b, ROWS), 0.0)
            row_mat[v, b * ROWS:(b + 1) * ROWS, :] = jnp.where(is_own, band, edge).astype(BF16)

    packed_at = lax.broadcasted_iota(jnp.int32, (2 * PACK, SLOTS * ROWS), 0)
    row_of = lax.broadcasted_iota(jnp.int32, (2 * PACK, SLOTS * ROWS), 1)
    place = jnp.where(packed_at < PACK, packed_at, packed_at - PACK)
    slot_of = ((place >= REACH).astype(jnp.int32) + (place >= 2 * REACH).astype(jnp.int32)
               + (place >= 3 * REACH).astype(jnp.int32))
    wanted = slot_of * (ROWS - REACH) + place + jnp.where(packed_at < PACK, 0, ROWS - REACH)
    pick_rows = (row_of == wanted).astype(F32).astype(BF16)
    local[0].wait()
    packed[...] = jnp.dot(pick_rows, own_rows[...].reshape(SLOTS * ROWS, SPAN),
                          preferred_element_type=F32).astype(BF16)

    pl.semaphore_wait(barrier, 1 + has_up.astype(jnp.int32) + has_down.astype(jnp.int32))

    for i in range(3):
        @pl.when(has_down)
        def _():
            down(i).start()

        @pl.when(has_up)
        def _():
            up(i).start()

    @pl.when(jnp.logical_not(has_up))
    def _():
        above[...] = jnp.zeros((PACK, SPAN), BF16)

    @pl.when(jnp.logical_not(has_down))
    def _():
        below[...] = jnp.zeros((PACK, SPAN), BF16)

    turned = lax.rem(REACH - tap + TILE, TILE)
    col_base = laid(col_taps, turned)
    row_at = lax.broadcasted_iota(jnp.int32, (TILE, TILE), 0)
    col_at = lax.broadcasted_iota(jnp.int32, (TILE, TILE), 1)
    near = jnp.abs(row_at - col_at) <= REACH
    for b in range(NB):
        band = rolled(col_base, b, TILE)
        col_mat[b * TILE:(b + 1) * TILE, :] = jnp.where(near, band, 0.0).astype(BF16)
        col_mat[(NB + b) * TILE:(NB + b + 1) * TILE, :] = jnp.where(near, 0.0, band).astype(BF16)

    local[1].wait()
    local[2].wait()
    turn = lax.rem(TILE - lax.rem(patch * SLOTS, TILE), TILE)
    sets = [pltpu.roll(coef_v[:, s, :], turn, 1) for s in range(SETS)]
    block = pltpu.roll(block_v[...], turn, 1)
    low_lanes = lax.broadcasted_iota(jnp.int32, (NB, TILE), 1) < TILE // 2

    def visit_scalars(home, v):
        visit = home * SLOTS + v
        scale = jnp.where(v < counts[home], ivar[visit], 0.0)
        inside = [jnp.where((t >= boxes[0, visit]) & (t < boxes[1, visit]), 1.0, 0.0) for t in range(TILES)]
        return scale, inside

    own = [visit_scalars(patch, v) for v in range(SLOTS)]
    other = [visit_scalars(before, v) for v in range(SLOTS)]
    chosen = []
    for t in range(TILES):
        pick = block[t:t + 1, :]
        total = jnp.zeros((NB, TILE), F32)
        for s in range(SETS):
            total = total + jnp.where(pick == s, sets[s], 0.0)
        chosen.append(total)
    for v in range(SLOTS):
        scale, inside = own[v]
        spread = [jnp.broadcast_to(chosen[t][:, v:v + 1], (NB, TILE)) * (scale * inside[t]) for t in range(TILES)]
        zero = jnp.zeros((NB, TILE), F32)
        for t in range(TILES):
            left = spread[t - 1] if t > 0 else zero
            right = spread[t + 1] if t + 1 < TILES else zero
            centre[t, v, 0:NB, :] = spread[t]
            beside[t, v, 0:NB, :] = jnp.where(low_lanes, left, right) * inside[t]

    def smooth(u):
        columns = pl.ds(pl.multiple_of(u * TILE, TILE), TILE)
        chunk = 256
        each = chunk // ROWS
        for at in range(NB * ROWS // chunk):
            mid, off = [None] * each, [None] * each
            for v in range(SLOTS):
                rows = pl.ds(16 * v, HALO)
                stack = jnp.concatenate([above[rows, columns], own_rows[v, :, columns], below[rows, columns]], axis=0)
                part = jnp.dot(row_mat[v, at * chunk:(at + 1) * chunk, :], stack, preferred_element_type=F32)
                for j in range(each):
                    b = at * each + j
                    term = part[j * ROWS:(j + 1) * ROWS, :]
                    one = term * centre[u, v, b:b + 1, :]
                    two = term * beside[u, v, b:b + 1, :]
                    mid[j] = one if mid[j] is None else mid[j] + one
                    off[j] = two if off[j] is None else off[j] + two
            for j in range(each):
                b = at * each + j
                lhs[u, :, b * TILE:(b + 1) * TILE] = mid[j].astype(BF16)
                side[u + 1, :, b * TILE:(b + 1) * TILE] = off[j].astype(BF16)

    low = lax.rem(lax.broadcasted_iota(jnp.int32, (ROWS, NB * TILE), 1), TILE) < TILE // 2

    def columns_of(first, count):
        for t in range(first, first + count):
            lhs[t, :, NB * TILE:] = jnp.where(low, side[t + 2], side[t])
        block_lhs = lhs[first:first + count].reshape(count * ROWS, 2 * NB * TILE)
        return jnp.dot(block_lhs, col_mat[...], preferred_element_type=F32)

    side[0] = jnp.zeros((ROWS, NB * TILE), BF16)
    side[TILES + 1] = jnp.zeros((ROWS, NB * TILE), BF16)

    def halo_wait(i):
        @pl.when(has_up)
        def _():
            down(i).wait_recv()

        @pl.when(has_down)
        def _():
            up(i).wait_recv()

    def far_copy(i):
        span = pl.ds((1 - i) * 2 * TILE, 2 * TILE)
        return pltpu.make_async_remote_copy(
            src_ref=far_out.at[:, span], dst_ref=far_in.at[:, span], send_sem=far_send.at[i], recv_sem=far_recv.at[i],
            device_id=(after, slab), device_id_type=MESH)

    for i, (top, count) in enumerate([(7, 3), (4, 2)]):
        halo_wait(i)
        lax.fori_loop(0, count, lambda k, c: (smooth(top - k), c)[1], 0)
        far = columns_of(6 - 2 * i, 2)
        for t in range(2):
            at = (2 - 2 * i + t) * TILE
            far_out[:, at:at + TILE] = far[t * ROWS:(t + 1) * ROWS].astype(BF16)
        far_copy(i).start()

    halo_wait(2)
    lax.fori_loop(0, 3, lambda i, c: (smooth(2 - i), c)[1], 0)
    near_part = columns_of(0, HALF)
    for t in reversed(range(HALF)):
        if t % 2 == 1:
            far_copy(1 - t // 2).wait_recv()
        weight = jnp.float32(0.0)
        for v in range(SLOTS):
            weight = weight + own[v][0] * own[v][1][t] + other[v][0] * other[v][1][t + HALF]
        total = near_part[t * ROWS:(t + 1) * ROWS] + far_in[:, t * TILE:(t + 1) * TILE].astype(F32)
        out[:, t * TILE:(t + 1) * TILE] = total / jnp.full((ROWS, TILE), jnp.maximum(weight, 1.0), F32)

    for i in range(2):
        far_copy(i).wait_send()
    for i in range(3):
        @pl.when(has_down)
        def _():
            down(i).wait_send()

        @pl.when(has_up)
        def _():
            up(i).wait_send()


def local_part(npatch, nslab, images, row_taps, col_taps, coef, blocks, boxes, ivar, counts):
    vmem = pl.BlockSpec(memory_space=pltpu.VMEM)
    smem = pl.BlockSpec(memory_space=pltpu.SMEM)
    anyplace = pl.BlockSpec(memory_space=pl.ANY)
    dma = pltpu.SemaphoreType.DMA
    return pl.pallas_call(
        functools.partial(kernel, npatch, nslab),
        out_shape=pltpu.VMEM((ROWS, HALF * TILE), F32),
        in_specs=[anyplace, vmem, vmem, anyplace, anyplace, smem, smem, smem],
        out_specs=vmem,
        scratch_shapes=[
            pltpu.VMEM((SLOTS, ROWS, SPAN), BF16),
            pltpu.VMEM((2 * PACK, SPAN), BF16),
            pltpu.VMEM((PACK, SPAN), BF16),
            pltpu.VMEM((PACK, SPAN), BF16),
            pltpu.VMEM((NB, SETS, TILE), F32),
            pltpu.VMEM((TILES, TILE), jnp.int32),
            pltpu.VMEM((SLOTS, NB * ROWS, DEPTH), BF16),
            pltpu.VMEM((2 * NB * TILE, TILE), BF16),
            pltpu.VMEM((TILES, SLOTS, 24, TILE), F32),
            pltpu.VMEM((TILES, SLOTS, 24, TILE), F32),
            pltpu.VMEM((TILES, ROWS, 2 * NB * TILE), BF16),
            pltpu.VMEM((TILES + 2, ROWS, NB * TILE), BF16),
            pltpu.VMEM((ROWS, HALF * TILE), BF16),
            pltpu.VMEM((ROWS, HALF * TILE), BF16),
            dma((3,)), dma((6,)), dma((6,)), dma((2,)), dma((2,)),
        ],
        compiler_params=pltpu.CompilerParams(
            collective_id=0, has_side_effects=True, vmem_limit_bytes=56 << 20),
        cost_estimate=pl.CostEstimate(flops=4_000_000_000, bytes_accessed=2_000_000, transcendentals=0),
    )(images, row_taps, col_taps, coef.transpose(2, 1, 0), blocks.T, boxes.T, ivar, counts)


def solution(mesh):
    return jax.shard_map(
        functools.partial(local_part, mesh.shape["ra"], mesh.shape["slab"]),
        mesh=mesh,
        in_specs=(P("ra", "slab", None), P(), P(), P(), P(), P(), P(), P()),
        out_specs=P("slab", "ra"),
        check_vma=False,
    )
```

```python
import functools

import jax
import jax.numpy as jnp
from jax import lax
from jax.experimental import pallas as pl
from jax.experimental.pallas import tpu as pltpu
from jax.sharding import PartitionSpec as P

MESH = pl.DeviceIdType.MESH
NB = 20
TAPS = 41
SETS = 4
REACH = 20
SLOTS = 4
ROWS = 64
EDGE = 32
NEAR = 24
TILE = 128
TILES = 8
HALF = 4
WIDE = HALF * TILE
F32 = jnp.float32
BF16 = jnp.bfloat16


def kernel(npatch, nslab, images, row_taps_in, col_taps_in, coef, blocks, boxes_in, ivar_in, counts_in,
           out, row_taps, col_taps, boxes, ivar, counts, window, coef_v, block_v, row_mat, col_mat, factor, mixed, far_out, far_in, near_out, near_in,
           tile_sem, local_sem, far_send, far_recv, near_send, near_recv):
    patch = lax.axis_index("ra")
    slab = lax.axis_index("slab")
    after = lax.rem(patch + 1, npatch)
    before = lax.rem(patch + npatch - 1, npatch)
    has_up = slab > 0
    has_down = slab < nslab - 1

    barrier = pltpu.get_barrier_semaphore()

    def greet(p, s):
        pl.semaphore_signal(barrier, inc=1, device_id=(p, s), device_id_type=MESH)

    tiles = [pltpu.make_async_copy(images.at[:, :, pl.ds(t * TILE, TILE)], window.at[t, :, :, pl.ds(0, TILE)],
                                   tile_sem.at[t]) for t in range(TILES)]
    lane_block = pl.ds(pl.multiple_of((patch * SLOTS // TILE) * TILE, TILE), TILE)
    small = [(col_taps_in, col_taps), (row_taps_in, row_taps), (boxes_in, boxes), (ivar_in, ivar), (counts_in, counts),
             (coef.at[:, :, lane_block], coef_v), (blocks.at[:, lane_block], block_v)]
    tables = [pltpu.make_async_copy(src, dst, local_sem.at[i]) for i, (src, dst) in enumerate(small)]
    for copy in tables + tiles[::-1]:
        copy.start()

    greet(before, slab)

    @pl.when(has_up)
    def _():
        greet(before, slab - 1)
        greet(patch, slab - 1)

    @pl.when(has_down)
    def _():
        greet(before, slab + 1)
        greet(patch, slab + 1)

    tap = lax.broadcasted_iota(jnp.int32, (TAPS, TILE), 0)
    lane = lax.broadcasted_iota(jnp.int32, (TAPS, TILE), 1)

    def laid(taps, at):
        return jnp.dot(taps[...], (lane == at).astype(F32).astype(BF16), preferred_element_type=F32)

    def rolled(base, b):
        band = jnp.broadcast_to(base[b:b + 1, :], (TILE, TILE))
        return pltpu.roll(band, 0, 1, stride=1, stride_axis=0)

    row_at = lax.broadcasted_iota(jnp.int32, (TILE, TILE), 0)
    col_at = lax.broadcasted_iota(jnp.int32, (TILE, TILE), 1)
    close = jnp.abs(row_at - col_at) <= REACH
    low_half = col_at < ROWS
    for copy in tables:
        copy.wait()
    col_base = laid(col_taps, lax.rem(REACH - tap + TILE, TILE))
    even_base = laid(row_taps, tap + (TILE - EDGE - REACH))
    odd_base = laid(row_taps, tap + (ROWS - EDGE - REACH))

    def build(pair):
        for b in (2 * pair, 2 * pair + 1):
            band = rolled(col_base, b)
            col_mat[0:TILE, b * TILE:(b + 1) * TILE] = jnp.where(close, band, 0.0).astype(BF16)
            col_mat[TILE:, b * TILE:(b + 1) * TILE] = jnp.where(close, 0.0, band).astype(BF16)
        both = jnp.where(low_half, rolled(even_base, 2 * pair), rolled(odd_base, 2 * pair + 1))
        row_mat[:, pair * TILE:(pair + 1) * TILE] = both.astype(BF16)

    def visit_scalars(home, v):
        visit = home * SLOTS + v
        scale = jnp.where(v < counts[home], ivar[visit], 0.0)
        inside = [jnp.where((t >= boxes[0, visit]) & (t < boxes[1, visit]), 1.0, 0.0) for t in range(TILES)]
        return scale, inside

    own = [visit_scalars(patch, v) for v in range(SLOTS)]
    other = [visit_scalars(before, v) for v in range(SLOTS)]
    turn = lax.rem(TILE - lax.rem(patch * SLOTS, TILE), TILE)
    sets = [pltpu.roll(coef_v[:, s, :], turn, 1) for s in range(SETS)]
    block = pltpu.roll(block_v[...], turn, 1)
    for t in range(TILES):
        pick = block[t:t + 1, :]
        chosen = jnp.zeros((NB, TILE), F32)
        for s in range(SETS):
            chosen = chosen + jnp.where(pick == s, sets[s], 0.0)
        for v in range(SLOTS):
            scale, inside = own[v]
            factor[t, v, 0:NB, :] = jnp.broadcast_to(chosen[:, v:v + 1], (NB, TILE)) * (scale * inside[t])

    @pl.when(jnp.logical_not(has_up))
    def _():
        far_in[0:EDGE, :] = jnp.zeros((EDGE, WIDE), BF16)
        near_in[0:NEAR, :] = jnp.zeros((NEAR, WIDE), F32)

    @pl.when(jnp.logical_not(has_down))
    def _():
        far_in[EDGE + ROWS:, :] = jnp.zeros((EDGE, WIDE), BF16)
        near_in[NEAR:, :] = jnp.zeros((NEAR, WIDE), F32)

    low = lax.broadcasted_iota(jnp.int32, (ROWS, TILE), 1) < TILE // 2

    def beside(t):
        for v in range(SLOTS):
            right = window[t + 1, v, :, 0:TILE] if t + 1 < TILES else jnp.zeros((ROWS, TILE), BF16)
            left = window[t - 1, v, :, 0:TILE] if t > 0 else jnp.zeros((ROWS, TILE), BF16)
            inside = own[v][1]
            keep = jnp.where(low, inside[t + 1] if t + 1 < TILES else 0.0, inside[t - 1] if t > 0 else 0.0)
            window[t, v, :, TILE:] = jnp.where(low, right, left) * keep.astype(BF16)

    def spread(first):
        for t in range(first, first + HALF):
            beside(t)

    def filtered(first, pairs, fresh):
        block_rows = window[first:first + HALF].reshape(HALF * SLOTS * ROWS, 2 * TILE)
        for pair in pairs:
            if fresh:
                build(pair)
            part = jnp.dot(block_rows, col_mat[:, pair * 2 * TILE:(pair + 1) * 2 * TILE], preferred_element_type=F32)
            for t in range(HALF):
                for w in range(2):
                    b = 2 * pair + w
                    total = None
                    for v in range(SLOTS):
                        at = (t * SLOTS + v) * ROWS
                        term = part[at:at + ROWS, w * TILE:(w + 1) * TILE] * factor[first + t, v, b:b + 1, :]
                        total = term if total is None else total + term
                    mixed[b * ROWS:(b + 1) * ROWS, t * TILE:(t + 1) * TILE] = total.astype(BF16)

    def row_product():
        return jnp.dot(row_mat[...], mixed[...], preferred_element_type=F32)

    def far_copy(i, p, s, src, dst, rows):
        return pltpu.make_async_remote_copy(
            src_ref=far_out.at[pl.ds(src, rows), :], dst_ref=far_in.at[pl.ds(dst, rows), :],
            send_sem=far_send.at[i], recv_sem=far_recv.at[i], device_id=(p, s), device_id_type=MESH)

    far_same = far_copy(0, after, slab, EDGE, EDGE, ROWS)
    far_up = far_copy(1, after, slab - 1, 0, EDGE + ROWS, EDGE)
    far_down = far_copy(2, after, slab + 1, EDGE + ROWS, 0, EDGE)

    def near_copy(i, s, src, dst):
        return pltpu.make_async_remote_copy(
            src_ref=near_out.at[pl.ds(src, NEAR), :], dst_ref=near_in.at[pl.ds(dst, NEAR), :],
            send_sem=near_send.at[i], recv_sem=near_recv.at[i], device_id=(patch, s), device_id_type=MESH)

    near_up = near_copy(0, slab - 1, 0, NEAR)
    near_down = near_copy(1, slab + 1, NEAR, 0)

    def send_to(target):
        @pl.when(slab == target)
        def _():
            far_same.start()

        @pl.when(slab == target + 1)
        def _():
            far_up.start()

        @pl.when(slab == target - 1)
        def _():
            far_down.start()

    for t in range(HALF - 1, TILES):
        tiles[t].wait()
    spread(HALF)
    filtered(HALF, range(NB // 2), True)
    far_out[...] = row_product().astype(BF16)
    links = has_up.astype(jnp.int32) + has_down.astype(jnp.int32)
    pl.semaphore_wait(barrier, 1 + 2 * links)
    send_to(1)
    for t in range(HALF - 1):
        tiles[t].wait()
    spread(0)
    filtered(0, range(0, 3), False)
    send_to(2)
    filtered(0, range(3, 6), False)
    send_to(3)
    filtered(0, range(6, 10), False)
    send_to(0)
    home = row_product()
    near_out[0:NEAR, :] = home[EDGE - NEAR:EDGE]
    near_out[NEAR:, :] = home[EDGE + ROWS:EDGE + ROWS + NEAR]

    @pl.when(has_up)
    def _():
        near_up.start()

    @pl.when(has_down)
    def _():
        near_down.start()

    out[...] = home[EDGE:EDGE + ROWS]

    @pl.when(has_up)
    def _():
        near_down.wait_recv()
        far_down.wait_recv()

    @pl.when(has_down)
    def _():
        near_up.wait_recv()
        far_up.wait_recv()

    far_same.wait_recv()
    for t in range(HALF):
        weight = jnp.float32(0.0)
        for v in range(SLOTS):
            weight = weight + own[v][0] * own[v][1][t] + other[v][0] * other[v][1][t + HALF]
        span = slice(t * TILE, (t + 1) * TILE)
        far_edges = jnp.concatenate([far_in[0:EDGE, span], far_in[EDGE + ROWS:, span]], axis=0).astype(F32)
        gap = jnp.zeros((ROWS - 2 * NEAR, TILE), F32)
        near_edges = jnp.concatenate([near_in[0:NEAR, span], gap, near_in[NEAR:, span]], axis=0)
        total = out[:, span] + near_edges + (far_in[EDGE:EDGE + ROWS, span].astype(F32) + far_edges)
        out[:, span] = total / jnp.full((ROWS, TILE), jnp.maximum(weight, 1.0), F32)

    far_same.wait_send()

    @pl.when(has_up)
    def _():
        far_up.wait_send()
        near_up.wait_send()

    @pl.when(has_down)
    def _():
        far_down.wait_send()
        near_down.wait_send()


def local_part(npatch, nslab, images, row_taps, col_taps, coef, blocks, boxes, ivar, counts):
    vmem = pl.BlockSpec(memory_space=pltpu.VMEM)
    anyplace = pl.BlockSpec(memory_space=pl.ANY)
    dma = pltpu.SemaphoreType.DMA
    return pl.pallas_call(
        functools.partial(kernel, npatch, nslab),
        out_shape=pltpu.VMEM((ROWS, WIDE), F32),
        in_specs=[anyplace] * 8,
        out_specs=vmem,
        scratch_shapes=[
            pltpu.VMEM(row_taps.shape, BF16),
            pltpu.VMEM(col_taps.shape, BF16),
            pltpu.SMEM(boxes.shape[::-1], jnp.int32),
            pltpu.SMEM(ivar.shape, F32),
            pltpu.SMEM(counts.shape, jnp.int32),
            pltpu.VMEM((TILES, SLOTS, ROWS, 2 * TILE), BF16),
            pltpu.VMEM((NB, SETS, TILE), F32),
            pltpu.VMEM((TILES, TILE), jnp.int32),
            pltpu.VMEM((TILE, NB * ROWS), BF16),
            pltpu.VMEM((2 * TILE, NB * TILE), BF16),
            pltpu.VMEM((TILES, SLOTS, 24, TILE), F32),
            pltpu.VMEM((NB * ROWS, WIDE), BF16),
            pltpu.VMEM((ROWS + 2 * EDGE, WIDE), BF16),
            pltpu.VMEM((ROWS + 2 * EDGE, WIDE), BF16),
            pltpu.VMEM((2 * NEAR, WIDE), F32),
            pltpu.VMEM((2 * NEAR, WIDE), F32),
            dma((TILES,)), dma((7,)), dma((3,)), dma((3,)), dma((2,)), dma((2,)),
        ],
        compiler_params=pltpu.CompilerParams(
            collective_id=0, has_side_effects=True, vmem_limit_bytes=56 << 20),
        cost_estimate=pl.CostEstimate(flops=4_000_000_000, bytes_accessed=2_000_000, transcendentals=0),
    )(images, row_taps, col_taps, coef.transpose(2, 1, 0), blocks.T, boxes.T, ivar, counts)


def solution(mesh):
    return jax.shard_map(
        functools.partial(local_part, mesh.shape["ra"], mesh.shape["slab"]),
        mesh=mesh,
        in_specs=(P("ra", "slab", None), P(), P(), P(), P(), P(), P(), P()),
        out_specs=P("slab", "ra"),
        check_vma=False,
    )
```

```python
import functools

import jax
import jax.numpy as jnp
from jax import lax
from jax.experimental import pallas as pl
from jax.experimental.pallas import tpu as pltpu
from jax.sharding import PartitionSpec as P

MESH = pl.DeviceIdType.MESH
NB = 20
TAPS = 41
SETS = 4
REACH = 20
SLOTS = 4
ROWS = 64
EDGE = 32
NEAR = 24
WHOLE = 16
REST = REACH - WHOLE
TILE = 128
TILES = 8
HALF = 4
WIDE = HALF * TILE
F32 = jnp.float32
BF16 = jnp.bfloat16


def kernel(npatch, nslab, images, row_taps_in, col_taps_in, coef, blocks, boxes_in, ivar_in, counts_in,
           out, row_taps, col_taps, boxes, ivar, counts, window, coef_v, block_v, row_mat, col_mat, factor, mixed, far_out, far_in, edge_out, edge_in, near_out, near_in,
           tile_sem, local_sem, far_send, far_recv, near_send, near_recv):
    patch = lax.axis_index("ra")
    slab = lax.axis_index("slab")
    after = lax.rem(patch + 1, npatch)
    before = lax.rem(patch + npatch - 1, npatch)
    has_up = slab > 0
    has_down = slab < nslab - 1

    barrier = pltpu.get_barrier_semaphore()

    def greet(p, s):
        pl.semaphore_signal(barrier, inc=1, device_id=(p, s), device_id_type=MESH)

    tiles = [pltpu.make_async_copy(images.at[:, :, pl.ds(t * TILE, TILE)], window.at[t, :, :, pl.ds(0, TILE)],
                                   tile_sem.at[t]) for t in range(TILES)]
    lane_block = pl.ds(pl.multiple_of((patch * SLOTS // TILE) * TILE, TILE), TILE)
    small = [(col_taps_in, col_taps), (row_taps_in, row_taps), (boxes_in, boxes), (ivar_in, ivar), (counts_in, counts),
             (coef.at[:, :, lane_block], coef_v), (blocks.at[:, lane_block], block_v)]
    tables = [pltpu.make_async_copy(src, dst, local_sem.at[i]) for i, (src, dst) in enumerate(small)]
    for copy in tables[:2] + tiles[:HALF - 2:-1] + tables[2:] + tiles[HALF - 2::-1]:
        copy.start()

    greet(before, slab)

    @pl.when(has_up)
    def _():
        greet(before, slab - 1)
        greet(patch, slab - 1)

    @pl.when(has_down)
    def _():
        greet(before, slab + 1)
        greet(patch, slab + 1)

    tap = lax.broadcasted_iota(jnp.int32, (TAPS, TILE), 0)
    lane = lax.broadcasted_iota(jnp.int32, (TAPS, TILE), 1)

    def laid(taps, at):
        return jnp.dot(taps[...], (lane == at).astype(F32).astype(BF16), preferred_element_type=F32)

    def rolled(base, b):
        band = jnp.broadcast_to(base[b:b + 1, :], (TILE, TILE))
        return pltpu.roll(band, 0, 1, stride=1, stride_axis=0)

    row_at = lax.broadcasted_iota(jnp.int32, (TILE, TILE), 0)
    col_at = lax.broadcasted_iota(jnp.int32, (TILE, TILE), 1)
    close = jnp.abs(row_at - col_at) <= REACH
    low_half = col_at < ROWS
    for copy in tables:
        copy.wait()
    col_base = laid(col_taps, lax.rem(REACH - tap + TILE, TILE))
    even_base = laid(row_taps, tap + (TILE - EDGE - REACH))
    odd_base = laid(row_taps, tap + (ROWS - EDGE - REACH))

    def build(pair):
        for b in (2 * pair, 2 * pair + 1):
            band = rolled(col_base, b)
            col_mat[0:TILE, b * TILE:(b + 1) * TILE] = jnp.where(close, band, 0.0).astype(BF16)
            col_mat[TILE:, b * TILE:(b + 1) * TILE] = jnp.where(close, 0.0, band).astype(BF16)
        both = jnp.where(low_half, rolled(even_base, 2 * pair), rolled(odd_base, 2 * pair + 1))
        row_mat[:, pair * TILE:(pair + 1) * TILE] = both.astype(BF16)

    def visit_scalars(home, v):
        visit = home * SLOTS + v
        scale = jnp.where(v < counts[home], ivar[visit], 0.0)
        inside = [jnp.where((t >= boxes[0, visit]) & (t < boxes[1, visit]), 1.0, 0.0) for t in range(TILES)]
        return scale, inside

    own = [visit_scalars(patch, v) for v in range(SLOTS)]
    other = [visit_scalars(before, v) for v in range(SLOTS)]
    turn = lax.rem(TILE - lax.rem(patch * SLOTS, TILE), TILE)
    sets = [pltpu.roll(coef_v[:, s, :], turn, 1) for s in range(SETS)]
    block = pltpu.roll(block_v[...], turn, 1)
    for t in range(TILES):
        pick = block[t:t + 1, :]
        chosen = jnp.zeros((NB, TILE), F32)
        for s in range(SETS):
            chosen = chosen + jnp.where(pick == s, sets[s], 0.0)
        for v in range(SLOTS):
            scale, inside = own[v]
            factor[t, v, 0:NB, :] = jnp.broadcast_to(chosen[:, v:v + 1], (NB, TILE)) * (scale * inside[t])

    @pl.when(jnp.logical_not(has_up))
    def _():
        edge_in[0] = jnp.zeros((WHOLE, WIDE + TILE), BF16)
        near_in[0:NEAR, :] = jnp.zeros((NEAR, WIDE), F32)

    @pl.when(jnp.logical_not(has_down))
    def _():
        edge_in[1] = jnp.zeros((WHOLE, WIDE + TILE), BF16)
        near_in[NEAR:, :] = jnp.zeros((NEAR, WIDE), F32)

    low = lax.broadcasted_iota(jnp.int32, (ROWS, TILE), 1) < TILE // 2

    def beside(t):
        for v in range(SLOTS):
            right = window[t + 1, v, :, 0:TILE] if t + 1 < TILES else jnp.zeros((ROWS, TILE), BF16)
            left = window[t - 1, v, :, 0:TILE] if t > 0 else jnp.zeros((ROWS, TILE), BF16)
            inside = own[v][1]
            keep = jnp.where(low, inside[t + 1] if t + 1 < TILES else 0.0, inside[t - 1] if t > 0 else 0.0)
            window[t, v, :, TILE:] = jnp.where(low, right, left) * keep.astype(BF16)

    def spread(first):
        for t in range(first, first + HALF):
            beside(t)

    def filtered(first, pairs, fresh):
        block_rows = window[first:first + HALF].reshape(HALF * SLOTS * ROWS, 2 * TILE)
        for pair in pairs:
            if fresh:
                build(pair)
            part = jnp.dot(block_rows, col_mat[:, pair * 2 * TILE:(pair + 1) * 2 * TILE], preferred_element_type=F32)
            for t in range(HALF):
                for w in range(2):
                    b = 2 * pair + w
                    total = None
                    for v in range(SLOTS):
                        at = (t * SLOTS + v) * ROWS
                        term = part[at:at + ROWS, w * TILE:(w + 1) * TILE] * factor[first + t, v, b:b + 1, :]
                        total = term if total is None else total + term
                    mixed[b * ROWS:(b + 1) * ROWS, t * TILE:(t + 1) * TILE] = total.astype(BF16)

    def row_product():
        return jnp.dot(row_mat[...], mixed[...], preferred_element_type=F32)

    def far_copy(i, p, s, src, dst):
        return pltpu.make_async_remote_copy(
            src_ref=src, dst_ref=dst, send_sem=far_send.at[i], recv_sem=far_recv.at[i],
            device_id=(p, s), device_id_type=MESH)

    far_same = far_copy(0, after, slab, far_out, far_in)
    far_up = far_copy(1, after, slab - 1, edge_out.at[0], edge_in.at[1])
    far_down = far_copy(2, after, slab + 1, edge_out.at[1], edge_in.at[0])

    def near_copy(i, s, src, dst):
        return pltpu.make_async_remote_copy(
            src_ref=near_out.at[pl.ds(src, NEAR), :], dst_ref=near_in.at[pl.ds(dst, NEAR), :],
            send_sem=near_send.at[i], recv_sem=near_recv.at[i], device_id=(patch, s), device_id_type=MESH)

    near_up = near_copy(0, slab - 1, 0, NEAR)
    near_down = near_copy(1, slab + 1, NEAR, 0)

    def send_to(target):
        @pl.when(slab == target)
        def _():
            far_same.start()

        @pl.when(slab == target + 1)
        def _():
            far_up.start()

        @pl.when(slab == target - 1)
        def _():
            far_down.start()

    for t in range(HALF - 1, TILES):
        tiles[t].wait()
    spread(HALF)
    filtered(HALF, range(NB // 2), True)
    far = row_product()
    far_out[...] = far[EDGE:EDGE + ROWS].astype(BF16)

    def edge(at, rest):
        last = [far[rest:rest + REST, t * TILE:(t + 1) * TILE] for t in range(HALF)]
        return jnp.concatenate([far[at:at + WHOLE], jnp.concatenate(last, axis=0)], axis=1).astype(BF16)

    edge_out[0] = edge(EDGE - WHOLE, EDGE - REACH)
    edge_out[1] = edge(EDGE + ROWS, EDGE + ROWS + WHOLE)
    links = has_up.astype(jnp.int32) + has_down.astype(jnp.int32)
    pl.semaphore_wait(barrier, 1 + 2 * links)
    send_to(1)
    for t in range(HALF - 1):
        tiles[t].wait()
    spread(0)
    filtered(0, range(0, 4), False)
    send_to(2)
    send_to(3)
    filtered(0, range(4, 10), False)
    send_to(0)
    home = row_product()
    near_out[0:NEAR, :] = home[EDGE - NEAR:EDGE]
    near_out[NEAR:, :] = home[EDGE + ROWS:EDGE + ROWS + NEAR]

    @pl.when(has_up)
    def _():
        near_up.start()

    @pl.when(has_down)
    def _():
        near_down.start()

    shares = []
    for t in range(HALF):
        weight = jnp.float32(0.0)
        for v in range(SLOTS):
            weight = weight + own[v][0] * own[v][1][t] + other[v][0] * other[v][1][t + HALF]
        shares.append(1.0 / jnp.full((ROWS, TILE), jnp.maximum(weight, 1.0), F32))

    @pl.when(has_up)
    def _():
        near_down.wait_recv()

    @pl.when(has_down)
    def _():
        near_up.wait_recv()

    out[0:NEAR, :] = home[EDGE:EDGE + NEAR] + near_in[0:NEAR, :]
    out[NEAR:ROWS - NEAR, :] = home[EDGE + NEAR:EDGE + ROWS - NEAR]
    out[ROWS - NEAR:, :] = home[EDGE + ROWS - NEAR:EDGE + ROWS] + near_in[NEAR:, :]

    @pl.when(has_up)
    def _():
        far_down.wait_recv()

    @pl.when(has_down)
    def _():
        far_up.wait_recv()

    far_same.wait_recv()
    for t in range(HALF):
        span = slice(t * TILE, (t + 1) * TILE)
        rest = slice(t * REST, (t + 1) * REST)
        ends = edge_in[:, :, span].astype(F32)
        last = edge_in[:, :, WIDE:].astype(F32)
        gap = jnp.zeros((ROWS - 2 * REACH, TILE), F32)
        edges = jnp.concatenate([ends[0], last[0, rest], gap, last[1, rest], ends[1]], axis=0)
        out[:, span] = (out[:, span] + (far_in[:, span].astype(F32) + edges)) * shares[t]

    far_same.wait_send()

    @pl.when(has_up)
    def _():
        far_up.wait_send()
        near_up.wait_send()

    @pl.when(has_down)
    def _():
        far_down.wait_send()
        near_down.wait_send()


def local_part(npatch, nslab, images, row_taps, col_taps, coef, blocks, boxes, ivar, counts):
    vmem = pl.BlockSpec(memory_space=pltpu.VMEM)
    anyplace = pl.BlockSpec(memory_space=pl.ANY)
    dma = pltpu.SemaphoreType.DMA
    return pl.pallas_call(
        functools.partial(kernel, npatch, nslab),
        out_shape=pltpu.VMEM((ROWS, WIDE), F32),
        in_specs=[anyplace] * 8,
        out_specs=vmem,
        scratch_shapes=[
            pltpu.VMEM(row_taps.shape, BF16),
            pltpu.VMEM(col_taps.shape, BF16),
            pltpu.SMEM(boxes.shape[::-1], jnp.int32),
            pltpu.SMEM(ivar.shape, F32),
            pltpu.SMEM(counts.shape, jnp.int32),
            pltpu.VMEM((TILES, SLOTS, ROWS, 2 * TILE), BF16),
            pltpu.VMEM((NB, SETS, TILE), F32),
            pltpu.VMEM((TILES, TILE), jnp.int32),
            pltpu.VMEM((TILE, NB * ROWS), BF16),
            pltpu.VMEM((2 * TILE, NB * TILE), BF16),
            pltpu.VMEM((TILES, SLOTS, 24, TILE), F32),
            pltpu.VMEM((NB * ROWS, WIDE), BF16),
            pltpu.VMEM((ROWS, WIDE), BF16),
            pltpu.VMEM((ROWS, WIDE), BF16),
            pltpu.VMEM((2, WHOLE, WIDE + TILE), BF16),
            pltpu.VMEM((2, WHOLE, WIDE + TILE), BF16),
            pltpu.VMEM((2 * NEAR, WIDE), F32),
            pltpu.VMEM((2 * NEAR, WIDE), F32),
            dma((TILES,)), dma((7,)), dma((3,)), dma((3,)), dma((2,)), dma((2,)),
        ],
        compiler_params=pltpu.CompilerParams(
            collective_id=0, has_side_effects=True, vmem_limit_bytes=56 << 20),
        cost_estimate=pl.CostEstimate(flops=4_000_000_000, bytes_accessed=2_000_000, transcendentals=0),
    )(images, row_taps, col_taps, coef.transpose(2, 1, 0), blocks.T, boxes.T, ivar, counts)


def solution(mesh):
    return jax.shard_map(
        functools.partial(local_part, mesh.shape["ra"], mesh.shape["slab"]),
        mesh=mesh,
        in_specs=(P("ra", "slab", None), P(), P(), P(), P(), P(), P(), P()),
        out_specs=P("slab", "ra"),
        check_vma=False,
    )
```

```python
import functools

import jax
import jax.numpy as jnp
from jax import lax
from jax.experimental import pallas as pl
from jax.experimental.pallas import tpu as pltpu
from jax.sharding import PartitionSpec as P

MESH = pl.DeviceIdType.MESH
NB = 20
TAPS = 41
SETS = 4
REACH = 20
SLOTS = 4
ROWS = 64
EDGE = 32
NEAR = 24
WHOLE = 16
REST = REACH - WHOLE
TILE = 128
TILES = 8
HALF = 4
WIDE = HALF * TILE
F32 = jnp.float32
BF16 = jnp.bfloat16


def kernel(npatch, nslab, images, row_taps_in, col_taps_in, coef, blocks, boxes_in, ivar_in, counts_in,
           out, row_taps, col_taps, boxes, ivar, counts, window, coef_v, block_v, row_mat, col_mat, factor, mixed, far_out, far_in, edge_out, edge_in, near_out, near_in,
           tile_sem, local_sem, far_send, far_recv, near_send, near_recv):
    patch = lax.axis_index("ra")
    slab = lax.axis_index("slab")
    after = lax.rem(patch + 1, npatch)
    before = lax.rem(patch + npatch - 1, npatch)
    has_up = slab > 0
    has_down = slab < nslab - 1

    barrier = pltpu.get_barrier_semaphore()

    def greet(p, s):
        pl.semaphore_signal(barrier, inc=1, device_id=(p, s), device_id_type=MESH)

    tiles = [pltpu.make_async_copy(images.at[:, :, pl.ds(t * TILE, TILE)], window.at[t, :, :, pl.ds(0, TILE)],
                                   tile_sem.at[t]) for t in range(TILES)]
    lane_block = pl.ds(pl.multiple_of((patch * SLOTS // TILE) * TILE, TILE), TILE)
    small = [(col_taps_in, col_taps), (row_taps_in, row_taps), (boxes_in, boxes), (ivar_in, ivar), (counts_in, counts),
             (coef.at[:, :, lane_block], coef_v), (blocks.at[:, lane_block], block_v)]
    tables = [pltpu.make_async_copy(src, dst, local_sem.at[i]) for i, (src, dst) in enumerate(small)]
    for copy in tables[:2] + tiles[:HALF - 2:-1] + tables[2:] + tiles[HALF - 2::-1]:
        copy.start()

    greet(before, slab)

    @pl.when(has_up)
    def _():
        greet(before, slab - 1)
        greet(patch, slab - 1)

    @pl.when(has_down)
    def _():
        greet(before, slab + 1)
        greet(patch, slab + 1)

    tap = lax.broadcasted_iota(jnp.int32, (TAPS, TILE), 0)
    lane = lax.broadcasted_iota(jnp.int32, (TAPS, TILE), 1)

    def laid(taps, at):
        return jnp.dot(taps[...], (lane == at).astype(F32).astype(BF16), preferred_element_type=F32)

    def rolled(base, b):
        band = jnp.broadcast_to(base[b:b + 1, :], (TILE, TILE))
        return pltpu.roll(band, 0, 1, stride=1, stride_axis=0)

    row_at = lax.broadcasted_iota(jnp.int32, (TILE, TILE), 0)
    col_at = lax.broadcasted_iota(jnp.int32, (TILE, TILE), 1)
    close = jnp.abs(row_at - col_at) <= REACH
    low_half = col_at < ROWS
    for copy in tables:
        copy.wait()
    col_base = laid(col_taps, lax.rem(REACH - tap + TILE, TILE))
    even_base = laid(row_taps, tap + (TILE - EDGE - REACH))
    odd_base = laid(row_taps, tap + (ROWS - EDGE - REACH))

    def build(pair):
        for b in (2 * pair, 2 * pair + 1):
            band = rolled(col_base, b)
            col_mat[0:TILE, b * TILE:(b + 1) * TILE] = jnp.where(close, band, 0.0).astype(BF16)
            col_mat[TILE:, b * TILE:(b + 1) * TILE] = jnp.where(close, 0.0, band).astype(BF16)
        both = jnp.where(low_half, rolled(even_base, 2 * pair), rolled(odd_base, 2 * pair + 1))
        row_mat[:, pair * TILE:(pair + 1) * TILE] = both.astype(BF16)

    def visit_scalars(home, v):
        visit = home * SLOTS + v
        scale = jnp.where(v < counts[home], ivar[visit], 0.0)
        inside = [jnp.where((t >= boxes[0, visit]) & (t < boxes[1, visit]), 1.0, 0.0) for t in range(TILES)]
        return scale, inside

    own = [visit_scalars(patch, v) for v in range(SLOTS)]
    other = [visit_scalars(before, v) for v in range(SLOTS)]
    turn = lax.rem(TILE - lax.rem(patch * SLOTS, TILE), TILE)
    sets = [pltpu.roll(coef_v[:, s, :], turn, 1) for s in range(SETS)]
    block = pltpu.roll(block_v[...], turn, 1)
    for t in range(TILES):
        pick = block[t:t + 1, :]
        chosen = jnp.zeros((NB, TILE), F32)
        for s in range(SETS):
            chosen = chosen + jnp.where(pick == s, sets[s], 0.0)
        for v in range(SLOTS):
            scale, inside = own[v]
            factor[t, v, 0:NB, :] = jnp.broadcast_to(chosen[:, v:v + 1], (NB, TILE)) * (scale * inside[t])

    @pl.when(jnp.logical_not(has_up))
    def _():
        edge_in[0] = jnp.zeros((WHOLE, WIDE + TILE), BF16)
        near_in[0:NEAR, :] = jnp.zeros((NEAR, WIDE), F32)

    @pl.when(jnp.logical_not(has_down))
    def _():
        edge_in[1] = jnp.zeros((WHOLE, WIDE + TILE), BF16)
        near_in[NEAR:, :] = jnp.zeros((NEAR, WIDE), F32)

    low = lax.broadcasted_iota(jnp.int32, (ROWS, TILE), 1) < TILE // 2

    def beside(t):
        for v in range(SLOTS):
            right = window[t + 1, v, :, 0:TILE] if t + 1 < TILES else jnp.zeros((ROWS, TILE), BF16)
            left = window[t - 1, v, :, 0:TILE] if t > 0 else jnp.zeros((ROWS, TILE), BF16)
            inside = own[v][1]
            keep = jnp.where(low, inside[t + 1] if t + 1 < TILES else 0.0, inside[t - 1] if t > 0 else 0.0)
            window[t, v, :, TILE:] = jnp.where(low, right, left) * keep.astype(BF16)

    def spread(first):
        for t in range(first, first + HALF):
            beside(t)

    def filtered(first, pairs, fresh):
        block_rows = window[first:first + HALF].reshape(HALF * SLOTS * ROWS, 2 * TILE)
        for pair in pairs:
            if fresh:
                build(pair)
            part = jnp.dot(block_rows, col_mat[:, pair * 2 * TILE:(pair + 1) * 2 * TILE], preferred_element_type=F32)
            for t in range(HALF):
                for w in range(2):
                    b = 2 * pair + w
                    total = None
                    for v in range(SLOTS):
                        at = (t * SLOTS + v) * ROWS
                        term = part[at:at + ROWS, w * TILE:(w + 1) * TILE] * factor[first + t, v, b:b + 1, :]
                        total = term if total is None else total + term
                    mixed[b * ROWS:(b + 1) * ROWS, t * TILE:(t + 1) * TILE] = total.astype(BF16)

    def row_product():
        return jnp.dot(row_mat[...], mixed[...], preferred_element_type=F32)

    def far_copy(i, p, s, src, dst):
        return pltpu.make_async_remote_copy(
            src_ref=src, dst_ref=dst, send_sem=far_send.at[i], recv_sem=far_recv.at[i],
            device_id=(p, s), device_id_type=MESH)

    far_same = far_copy(0, after, slab, far_out, far_in)
    far_up = far_copy(1, after, slab - 1, edge_out.at[0], edge_in.at[1])
    far_down = far_copy(2, after, slab + 1, edge_out.at[1], edge_in.at[0])

    def near_copy(i, s, src, dst):
        return pltpu.make_async_remote_copy(
            src_ref=near_out.at[pl.ds(src, NEAR), :], dst_ref=near_in.at[pl.ds(dst, NEAR), :],
            send_sem=near_send.at[i], recv_sem=near_recv.at[i], device_id=(patch, s), device_id_type=MESH)

    near_up = near_copy(0, slab - 1, 0, NEAR)
    near_down = near_copy(1, slab + 1, NEAR, 0)

    def send_to(target):
        if target != 1:
            @pl.when(slab == target)
            def _():
                far_same.start()

        @pl.when(slab == target + 1)
        def _():
            far_up.start()

        @pl.when(slab == target - 1)
        def _():
            far_down.start()

    for t in range(HALF - 1, TILES):
        tiles[t].wait()
    spread(HALF)
    filtered(HALF, range(NB // 2), True)
    far = row_product()
    far_out[...] = far[EDGE:EDGE + ROWS].astype(BF16)

    links = has_up.astype(jnp.int32) + has_down.astype(jnp.int32)
    pl.semaphore_wait(barrier, 1 + 2 * links)

    @pl.when(slab == 1)
    def _():
        far_same.start()

    def edge(at, rest):
        last = [far[rest:rest + REST, t * TILE:(t + 1) * TILE] for t in range(HALF)]
        return jnp.concatenate([far[at:at + WHOLE], jnp.concatenate(last, axis=0)], axis=1).astype(BF16)

    edge_out[0] = edge(EDGE - WHOLE, EDGE - REACH)
    edge_out[1] = edge(EDGE + ROWS, EDGE + ROWS + WHOLE)
    send_to(1)
    for t in range(HALF - 1):
        tiles[t].wait()
    spread(0)
    filtered(0, range(0, 3), False)
    send_to(2)
    send_to(3)
    filtered(0, range(3, 10), False)
    send_to(0)
    home = row_product()
    near_out[0:NEAR, :] = home[EDGE - NEAR:EDGE]
    near_out[NEAR:, :] = home[EDGE + ROWS:EDGE + ROWS + NEAR]

    @pl.when(has_up)
    def _():
        near_up.start()

    @pl.when(has_down)
    def _():
        near_down.start()

    shares = []
    for t in range(HALF):
        weight = jnp.float32(0.0)
        for v in range(SLOTS):
            weight = weight + own[v][0] * own[v][1][t] + other[v][0] * other[v][1][t + HALF]
        shares.append(1.0 / jnp.full((ROWS, TILE), jnp.maximum(weight, 1.0), F32))

    @pl.when(has_up)
    def _():
        near_down.wait_recv()

    @pl.when(has_down)
    def _():
        near_up.wait_recv()

    out[0:NEAR, :] = home[EDGE:EDGE + NEAR] + near_in[0:NEAR, :]
    out[NEAR:ROWS - NEAR, :] = home[EDGE + NEAR:EDGE + ROWS - NEAR]
    out[ROWS - NEAR:, :] = home[EDGE + ROWS - NEAR:EDGE + ROWS] + near_in[NEAR:, :]

    @pl.when(has_up)
    def _():
        far_down.wait_recv()

    @pl.when(has_down)
    def _():
        far_up.wait_recv()

    far_same.wait_recv()
    for t in range(HALF):
        span = slice(t * TILE, (t + 1) * TILE)
        rest = slice(t * REST, (t + 1) * REST)
        ends = edge_in[:, :, span].astype(F32)
        last = edge_in[:, :, WIDE:].astype(F32)
        gap = jnp.zeros((ROWS - 2 * REACH, TILE), F32)
        edges = jnp.concatenate([ends[0], last[0, rest], gap, last[1, rest], ends[1]], axis=0)
        out[:, span] = (out[:, span] + (far_in[:, span].astype(F32) + edges)) * shares[t]

    far_same.wait_send()

    @pl.when(has_up)
    def _():
        far_up.wait_send()
        near_up.wait_send()

    @pl.when(has_down)
    def _():
        far_down.wait_send()
        near_down.wait_send()


def local_part(npatch, nslab, images, row_taps, col_taps, coef, blocks, boxes, ivar, counts):
    vmem = pl.BlockSpec(memory_space=pltpu.VMEM)
    anyplace = pl.BlockSpec(memory_space=pl.ANY)
    dma = pltpu.SemaphoreType.DMA
    return pl.pallas_call(
        functools.partial(kernel, npatch, nslab),
        out_shape=pltpu.VMEM((ROWS, WIDE), F32),
        in_specs=[anyplace] * 8,
        out_specs=vmem,
        scratch_shapes=[
            pltpu.VMEM(row_taps.shape, BF16),
            pltpu.VMEM(col_taps.shape, BF16),
            pltpu.SMEM(boxes.shape[::-1], jnp.int32),
            pltpu.SMEM(ivar.shape, F32),
            pltpu.SMEM(counts.shape, jnp.int32),
            pltpu.VMEM((TILES, SLOTS, ROWS, 2 * TILE), BF16),
            pltpu.VMEM((NB, SETS, TILE), F32),
            pltpu.VMEM((TILES, TILE), jnp.int32),
            pltpu.VMEM((TILE, NB * ROWS), BF16),
            pltpu.VMEM((2 * TILE, NB * TILE), BF16),
            pltpu.VMEM((TILES, SLOTS, 24, TILE), F32),
            pltpu.VMEM((NB * ROWS, WIDE), BF16),
            pltpu.VMEM((ROWS, WIDE), BF16),
            pltpu.VMEM((ROWS, WIDE), BF16),
            pltpu.VMEM((2, WHOLE, WIDE + TILE), BF16),
            pltpu.VMEM((2, WHOLE, WIDE + TILE), BF16),
            pltpu.VMEM((2 * NEAR, WIDE), F32),
            pltpu.VMEM((2 * NEAR, WIDE), F32),
            dma((TILES,)), dma((7,)), dma((3,)), dma((3,)), dma((2,)), dma((2,)),
        ],
        compiler_params=pltpu.CompilerParams(
            collective_id=0, has_side_effects=True, vmem_limit_bytes=56 << 20),
        cost_estimate=pl.CostEstimate(flops=4_000_000_000, bytes_accessed=2_000_000, transcendentals=0),
    )(images, row_taps, col_taps, coef.transpose(2, 1, 0), blocks.T, boxes.T, ivar, counts)


def solution(mesh):
    return jax.shard_map(
        functools.partial(local_part, mesh.shape["ra"], mesh.shape["slab"]),
        mesh=mesh,
        in_specs=(P("ra", "slab", None), P(), P(), P(), P(), P(), P(), P()),
        out_specs=P("slab", "ra"),
        check_vma=False,
    )
```

```python
import functools

import jax
import jax.numpy as jnp
from jax import lax
from jax.experimental import pallas as pl
from jax.experimental.pallas import tpu as pltpu
from jax.sharding import PartitionSpec as P

MESH = pl.DeviceIdType.MESH
NB = 20
TAPS = 41
SETS = 4
REACH = 20
SLOTS = 4
ROWS = 64
EDGE = 32
NEAR = 24
WHOLE = 16
REST = REACH - WHOLE
TILE = 128
TILES = 8
HALF = 4
WIDE = HALF * TILE
F32 = jnp.float32
BF16 = jnp.bfloat16


def kernel(npatch, nslab, images, row_taps_in, col_taps_in, coef, blocks, boxes_in, ivar_in, counts_in,
           out, row_taps, col_taps, boxes, ivar, counts, window, coef_v, block_v, row_mat, col_mat, factor, mixed, far_out, far_in, edge_out, edge_in, near_out, near_in,
           tile_sem, local_sem, far_send, far_recv, near_send, near_recv):
    patch = lax.axis_index("ra")
    slab = lax.axis_index("slab")
    after = lax.rem(patch + 1, npatch)
    before = lax.rem(patch + npatch - 1, npatch)
    has_up = slab > 0
    has_down = slab < nslab - 1

    barrier = pltpu.get_barrier_semaphore()

    def greet(p, s):
        pl.semaphore_signal(barrier, inc=1, device_id=(p, s), device_id_type=MESH)

    tiles = [pltpu.make_async_copy(images.at[:, :, pl.ds(t * TILE, TILE)], window.at[t, :, :, pl.ds(0, TILE)],
                                   tile_sem.at[t]) for t in range(TILES)]
    lane_block = pl.ds(pl.multiple_of((patch * SLOTS // TILE) * TILE, TILE), TILE)
    small = [(col_taps_in, col_taps), (row_taps_in, row_taps), (boxes_in, boxes), (ivar_in, ivar), (counts_in, counts),
             (coef.at[:, :, lane_block], coef_v), (blocks.at[:, lane_block], block_v)]
    tables = [pltpu.make_async_copy(src, dst, local_sem.at[i]) for i, (src, dst) in enumerate(small)]
    for copy in tables[:2] + tiles[:HALF - 2:-1] + tables[2:] + tiles[HALF - 2::-1]:
        copy.start()

    greet(before, slab)

    @pl.when(has_up)
    def _():
        greet(before, slab - 1)
        greet(patch, slab - 1)

    @pl.when(has_down)
    def _():
        greet(before, slab + 1)
        greet(patch, slab + 1)

    tap = lax.broadcasted_iota(jnp.int32, (TAPS, TILE), 0)
    lane = lax.broadcasted_iota(jnp.int32, (TAPS, TILE), 1)

    def laid(taps, at):
        return jnp.dot(taps[...], (lane == at).astype(F32).astype(BF16), preferred_element_type=F32)

    def rolled(base, b):
        band = jnp.broadcast_to(base[b:b + 1, :], (TILE, TILE))
        return pltpu.roll(band, 0, 1, stride=1, stride_axis=0)

    row_at = lax.broadcasted_iota(jnp.int32, (TILE, TILE), 0)
    col_at = lax.broadcasted_iota(jnp.int32, (TILE, TILE), 1)
    close = jnp.abs(row_at - col_at) <= REACH
    low_half = col_at < ROWS
    for copy in tables + tiles[HALF - 1:]:
        copy.wait()
    col_base = laid(col_taps, lax.rem(REACH - tap + TILE, TILE))
    even_base = laid(row_taps, tap + (TILE - EDGE - REACH))
    odd_base = laid(row_taps, tap + (ROWS - EDGE - REACH))

    def build(pair):
        for b in (2 * pair, 2 * pair + 1):
            band = rolled(col_base, b)
            col_mat[0:TILE, b * TILE:(b + 1) * TILE] = jnp.where(close, band, 0.0).astype(BF16)
            col_mat[TILE:, b * TILE:(b + 1) * TILE] = jnp.where(close, 0.0, band).astype(BF16)
        both = jnp.where(low_half, rolled(even_base, 2 * pair), rolled(odd_base, 2 * pair + 1))
        row_mat[:, pair * TILE:(pair + 1) * TILE] = both.astype(BF16)

    def visit_scalars(home, v):
        visit = home * SLOTS + v
        scale = jnp.where(v < counts[home], ivar[visit], 0.0)
        inside = [jnp.where((t >= boxes[0, visit]) & (t < boxes[1, visit]), 1.0, 0.0) for t in range(TILES)]
        return scale, inside

    own = [visit_scalars(patch, v) for v in range(SLOTS)]
    turn = lax.rem(TILE - lax.rem(patch * SLOTS, TILE), TILE)
    sets = [pltpu.roll(coef_v[:, s, :], turn, 1) for s in range(SETS)]
    block = pltpu.roll(block_v[...], turn, 1)

    def factors(first):
        for t in range(first, first + HALF):
            pick = block[t:t + 1, :]
            chosen = jnp.zeros((NB, TILE), F32)
            for s in range(SETS):
                chosen = chosen + jnp.where(pick == s, sets[s], 0.0)
            for v in range(SLOTS):
                scale, inside = own[v]
                factor[t, v, 0:NB, :] = jnp.broadcast_to(chosen[:, v:v + 1], (NB, TILE)) * (scale * inside[t])

    factors(HALF)

    @pl.when(jnp.logical_not(has_up))
    def _():
        edge_in[0] = jnp.zeros((WHOLE, WIDE + TILE), BF16)
        near_in[0:NEAR, :] = jnp.zeros((NEAR, WIDE), F32)

    @pl.when(jnp.logical_not(has_down))
    def _():
        edge_in[1] = jnp.zeros((WHOLE, WIDE + TILE), BF16)
        near_in[NEAR:, :] = jnp.zeros((NEAR, WIDE), F32)

    low = lax.broadcasted_iota(jnp.int32, (ROWS, TILE), 1) < TILE // 2

    def beside(t):
        for v in range(SLOTS):
            right = window[t + 1, v, :, 0:TILE] if t + 1 < TILES else jnp.zeros((ROWS, TILE), BF16)
            left = window[t - 1, v, :, 0:TILE] if t > 0 else jnp.zeros((ROWS, TILE), BF16)
            inside = own[v][1]
            keep = jnp.where(low, inside[t + 1] if t + 1 < TILES else 0.0, inside[t - 1] if t > 0 else 0.0)
            window[t, v, :, TILE:] = jnp.where(low, right, left) * keep.astype(BF16)

    def spread(first):
        for t in range(first, first + HALF):
            beside(t)

    def filtered(first, pairs, fresh):
        block_rows = window[first:first + HALF].reshape(HALF * SLOTS * ROWS, 2 * TILE)
        for pair in pairs:
            if fresh:
                build(pair)
            part = jnp.dot(block_rows, col_mat[:, pair * 2 * TILE:(pair + 1) * 2 * TILE], preferred_element_type=F32)
            for t in range(HALF):
                for w in range(2):
                    b = 2 * pair + w
                    total = None
                    for v in range(SLOTS):
                        at = (t * SLOTS + v) * ROWS
                        term = part[at:at + ROWS, w * TILE:(w + 1) * TILE] * factor[first + t, v, b:b + 1, :]
                        total = term if total is None else total + term
                    mixed[b * ROWS:(b + 1) * ROWS, t * TILE:(t + 1) * TILE] = total.astype(BF16)

    def row_product():
        return jnp.dot(row_mat[...], mixed[...], preferred_element_type=F32)

    def far_copy(i, p, s, src, dst):
        return pltpu.make_async_remote_copy(
            src_ref=src, dst_ref=dst, send_sem=far_send.at[i], recv_sem=far_recv.at[i],
            device_id=(p, s), device_id_type=MESH)

    far_same = far_copy(0, after, slab, far_out, far_in)
    far_up = far_copy(1, after, slab - 1, edge_out.at[0], edge_in.at[1])
    far_down = far_copy(2, after, slab + 1, edge_out.at[1], edge_in.at[0])

    def near_copy(i, s, src, dst):
        return pltpu.make_async_remote_copy(
            src_ref=near_out.at[pl.ds(src, NEAR), :], dst_ref=near_in.at[pl.ds(dst, NEAR), :],
            send_sem=near_send.at[i], recv_sem=near_recv.at[i], device_id=(patch, s), device_id_type=MESH)

    near_up = near_copy(0, slab - 1, 0, NEAR)
    near_down = near_copy(1, slab + 1, NEAR, 0)

    def send_to(target):
        if target != 1:
            @pl.when(slab == target)
            def _():
                far_same.start()

        @pl.when(slab == target + 1)
        def _():
            far_up.start()

        @pl.when(slab == target - 1)
        def _():
            far_down.start()

    spread(HALF)
    filtered(HALF, range(NB // 2), True)
    far = row_product()
    far_out[...] = far[EDGE:EDGE + ROWS].astype(BF16)

    links = has_up.astype(jnp.int32) + has_down.astype(jnp.int32)
    pl.semaphore_wait(barrier, 1 + 2 * links)

    @pl.when(slab == 1)
    def _():
        far_same.start()

    def edge(at, rest):
        last = [far[rest:rest + REST, t * TILE:(t + 1) * TILE] for t in range(HALF)]
        return jnp.concatenate([far[at:at + WHOLE], jnp.concatenate(last, axis=0)], axis=1).astype(BF16)

    edge_out[0] = edge(EDGE - WHOLE, EDGE - REACH)
    edge_out[1] = edge(EDGE + ROWS, EDGE + ROWS + WHOLE)
    send_to(1)
    for t in range(HALF - 1):
        tiles[t].wait()
    factors(0)
    spread(0)
    filtered(0, range(0, 3), False)
    send_to(2)
    send_to(3)
    filtered(0, range(3, 10), False)
    send_to(0)
    home = row_product()
    near_out[0:NEAR, :] = home[EDGE - NEAR:EDGE]
    near_out[NEAR:, :] = home[EDGE + ROWS:EDGE + ROWS + NEAR]

    @pl.when(has_up)
    def _():
        near_up.start()

    @pl.when(has_down)
    def _():
        near_down.start()

    other = [visit_scalars(before, v) for v in range(SLOTS)]
    shares = []
    for t in range(HALF):
        weight = jnp.float32(0.0)
        for v in range(SLOTS):
            weight = weight + own[v][0] * own[v][1][t] + other[v][0] * other[v][1][t + HALF]
        shares.append(1.0 / jnp.full((ROWS, TILE), jnp.maximum(weight, 1.0), F32))

    @pl.when(has_up)
    def _():
        near_down.wait_recv()

    @pl.when(has_down)
    def _():
        near_up.wait_recv()

    out[0:NEAR, :] = home[EDGE:EDGE + NEAR] + near_in[0:NEAR, :]
    out[NEAR:ROWS - NEAR, :] = home[EDGE + NEAR:EDGE + ROWS - NEAR]
    out[ROWS - NEAR:, :] = home[EDGE + ROWS - NEAR:EDGE + ROWS] + near_in[NEAR:, :]

    @pl.when(has_up)
    def _():
        far_down.wait_recv()

    @pl.when(has_down)
    def _():
        far_up.wait_recv()

    far_same.wait_recv()
    for t in range(HALF):
        span = slice(t * TILE, (t + 1) * TILE)
        rest = slice(t * REST, (t + 1) * REST)
        ends = edge_in[:, :, span].astype(F32)
        last = edge_in[:, :, WIDE:].astype(F32)
        gap = jnp.zeros((ROWS - 2 * REACH, TILE), F32)
        edges = jnp.concatenate([ends[0], last[0, rest], gap, last[1, rest], ends[1]], axis=0)
        out[:, span] = (out[:, span] + (far_in[:, span].astype(F32) + edges)) * shares[t]

    far_same.wait_send()

    @pl.when(has_up)
    def _():
        far_up.wait_send()
        near_up.wait_send()

    @pl.when(has_down)
    def _():
        far_down.wait_send()
        near_down.wait_send()


def local_part(npatch, nslab, images, row_taps, col_taps, coef, blocks, boxes, ivar, counts):
    vmem = pl.BlockSpec(memory_space=pltpu.VMEM)
    anyplace = pl.BlockSpec(memory_space=pl.ANY)
    dma = pltpu.SemaphoreType.DMA
    return pl.pallas_call(
        functools.partial(kernel, npatch, nslab),
        out_shape=pltpu.VMEM((ROWS, WIDE), F32),
        in_specs=[anyplace] * 8,
        out_specs=vmem,
        scratch_shapes=[
            pltpu.VMEM(row_taps.shape, BF16),
            pltpu.VMEM(col_taps.shape, BF16),
            pltpu.SMEM(boxes.shape[::-1], jnp.int32),
            pltpu.SMEM(ivar.shape, F32),
            pltpu.SMEM(counts.shape, jnp.int32),
            pltpu.VMEM((TILES, SLOTS, ROWS, 2 * TILE), BF16),
            pltpu.VMEM((NB, SETS, TILE), F32),
            pltpu.VMEM((TILES, TILE), jnp.int32),
            pltpu.VMEM((TILE, NB * ROWS), BF16),
            pltpu.VMEM((2 * TILE, NB * TILE), BF16),
            pltpu.VMEM((TILES, SLOTS, 24, TILE), F32),
            pltpu.VMEM((NB * ROWS, WIDE), BF16),
            pltpu.VMEM((ROWS, WIDE), BF16),
            pltpu.VMEM((ROWS, WIDE), BF16),
            pltpu.VMEM((2, WHOLE, WIDE + TILE), BF16),
            pltpu.VMEM((2, WHOLE, WIDE + TILE), BF16),
            pltpu.VMEM((2 * NEAR, WIDE), F32),
            pltpu.VMEM((2 * NEAR, WIDE), F32),
            dma((TILES,)), dma((7,)), dma((3,)), dma((3,)), dma((2,)), dma((2,)),
        ],
        compiler_params=pltpu.CompilerParams(
            collective_id=0, has_side_effects=True, vmem_limit_bytes=56 << 20),
        cost_estimate=pl.CostEstimate(flops=4_000_000_000, bytes_accessed=2_000_000, transcendentals=0),
    )(images, row_taps, col_taps, coef.transpose(2, 1, 0), blocks.T, boxes.T, ivar, counts)


def solution(mesh):
    return jax.shard_map(
        functools.partial(local_part, mesh.shape["ra"], mesh.shape["slab"]),
        mesh=mesh,
        in_specs=(P("ra", "slab", None), P(), P(), P(), P(), P(), P(), P()),
        out_specs=P("slab", "ra"),
        check_vma=False,
    )
```

```python
import functools

import jax
import jax.numpy as jnp
from jax import lax
from jax.experimental import pallas as pl
from jax.experimental.pallas import tpu as pltpu
from jax.sharding import PartitionSpec as P

MESH = pl.DeviceIdType.MESH
NB = 20
TAPS = 41
SETS = 4
REACH = 20
SLOTS = 4
ROWS = 64
EDGE = 32
NEAR = 24
WHOLE = 16
REST = REACH - WHOLE
TILE = 128
TILES = 8
HALF = 4
WIDE = HALF * TILE
F32 = jnp.float32
BF16 = jnp.bfloat16


def kernel(npatch, nslab, images, row_taps_in, col_taps_in, coef, blocks, boxes_in, ivar_in, counts_in,
           out, row_taps, col_taps, boxes, ivar, counts, window, coef_v, block_v, row_mat, col_mat, factor, mixed, far_out, far_in, edge_out, edge_in, near_out, near_in,
           tile_sem, local_sem, far_send, far_recv, near_send, near_recv):
    patch = lax.axis_index("ra")
    slab = lax.axis_index("slab")
    after = lax.rem(patch + 1, npatch)
    before = lax.rem(patch + npatch - 1, npatch)
    has_up = slab > 0
    has_down = slab < nslab - 1

    barrier = pltpu.get_barrier_semaphore()

    def greet(p, s):
        pl.semaphore_signal(barrier, inc=1, device_id=(p, s), device_id_type=MESH)

    tiles = [pltpu.make_async_copy(images.at[:, :, pl.ds(t * TILE, TILE)], window.at[t, :, :, pl.ds(0, TILE)],
                                   tile_sem.at[t]) for t in range(TILES)]
    lane_block = pl.ds(pl.multiple_of((patch * SLOTS // TILE) * TILE, TILE), TILE)
    small = [(col_taps_in, col_taps), (row_taps_in, row_taps), (boxes_in, boxes), (ivar_in, ivar), (counts_in, counts),
             (coef.at[:, :, lane_block], coef_v), (blocks.at[:, lane_block], block_v)]
    tables = [pltpu.make_async_copy(src, dst, local_sem.at[i]) for i, (src, dst) in enumerate(small)]
    for copy in tables[:2] + tiles[:HALF - 2:-1] + tables[2:] + tiles[HALF - 2::-1]:
        copy.start()

    greet(before, slab)

    @pl.when(has_up)
    def _():
        greet(before, slab - 1)
        greet(patch, slab - 1)

    @pl.when(has_down)
    def _():
        greet(before, slab + 1)
        greet(patch, slab + 1)

    tap = lax.broadcasted_iota(jnp.int32, (TAPS, TILE), 0)
    lane = lax.broadcasted_iota(jnp.int32, (TAPS, TILE), 1)

    def laid(taps, at):
        return jnp.dot(taps[...], (lane == at).astype(F32).astype(BF16), preferred_element_type=F32)

    def rolled(base, b):
        band = jnp.broadcast_to(base[b:b + 1, :], (TILE, TILE))
        return pltpu.roll(band, 0, 1, stride=1, stride_axis=0)

    row_at = lax.broadcasted_iota(jnp.int32, (TILE, TILE), 0)
    col_at = lax.broadcasted_iota(jnp.int32, (TILE, TILE), 1)
    close = jnp.abs(row_at - col_at) <= REACH
    low_half = col_at < ROWS
    for copy in tables + tiles[HALF - 1:]:
        copy.wait()
    col_base = laid(col_taps, lax.rem(REACH - tap + TILE, TILE))
    even_base = laid(row_taps, tap + (TILE - EDGE - REACH))
    odd_base = laid(row_taps, tap + (ROWS - EDGE - REACH))

    def build(pair):
        for b in (2 * pair, 2 * pair + 1):
            band = rolled(col_base, b)
            col_mat[0:TILE, b * TILE:(b + 1) * TILE] = jnp.where(close, band, 0.0).astype(BF16)
            col_mat[TILE:, b * TILE:(b + 1) * TILE] = jnp.where(close, 0.0, band).astype(BF16)
        both = jnp.where(low_half, rolled(even_base, 2 * pair), rolled(odd_base, 2 * pair + 1))
        row_mat[:, pair * TILE:(pair + 1) * TILE] = both.astype(BF16)

    def visit_scalars(home, v):
        visit = home * SLOTS + v
        scale = jnp.where(v < counts[home], ivar[visit], 0.0)
        inside = [jnp.where((t >= boxes[0, visit]) & (t < boxes[1, visit]), 1.0, 0.0) for t in range(TILES)]
        return scale, inside

    own = [visit_scalars(patch, v) for v in range(SLOTS)]
    turn = lax.rem(TILE - lax.rem(patch * SLOTS, TILE), TILE)
    sets = [pltpu.roll(coef_v[:, s, :], turn, 1) for s in range(SETS)]
    block = pltpu.roll(block_v[...], turn, 1)

    def factors(first):
        for t in range(first, first + HALF):
            pick = block[t:t + 1, :]
            chosen = jnp.zeros((NB, TILE), F32)
            for s in range(SETS):
                chosen = chosen + jnp.where(pick == s, sets[s], 0.0)
            for v in range(SLOTS):
                scale, inside = own[v]
                factor[t, v, 0:NB, :] = jnp.broadcast_to(chosen[:, v:v + 1], (NB, TILE)) * (scale * inside[t])

    factors(HALF)

    @pl.when(jnp.logical_not(has_up))
    def _():
        edge_in[0] = jnp.zeros((WHOLE, WIDE + TILE), BF16)
        near_in[0:NEAR, :] = jnp.zeros((NEAR, WIDE), F32)

    @pl.when(jnp.logical_not(has_down))
    def _():
        edge_in[1] = jnp.zeros((WHOLE, WIDE + TILE), BF16)
        near_in[NEAR:, :] = jnp.zeros((NEAR, WIDE), F32)

    low = lax.broadcasted_iota(jnp.int32, (ROWS, TILE), 1) < TILE // 2

    def beside(t):
        for v in range(SLOTS):
            right = window[t + 1, v, :, 0:TILE] if t + 1 < TILES else jnp.zeros((ROWS, TILE), BF16)
            left = window[t - 1, v, :, 0:TILE] if t > 0 else jnp.zeros((ROWS, TILE), BF16)
            inside = own[v][1]
            keep = jnp.where(low, inside[t + 1] if t + 1 < TILES else 0.0, inside[t - 1] if t > 0 else 0.0)
            window[t, v, :, TILE:] = jnp.where(low, right, left) * keep.astype(BF16)

    def spread(first):
        for t in range(first, first + HALF):
            beside(t)

    def filtered(first, pairs, fresh):
        block_rows = window[first:first + HALF].reshape(HALF * SLOTS * ROWS, 2 * TILE)
        for pair in pairs:
            if fresh:
                build(pair)
            part = jnp.dot(block_rows, col_mat[:, pair * 2 * TILE:(pair + 1) * 2 * TILE], preferred_element_type=F32)
            for t in range(HALF):
                for w in range(2):
                    b = 2 * pair + w
                    total = None
                    for v in range(SLOTS):
                        at = (t * SLOTS + v) * ROWS
                        term = part[at:at + ROWS, w * TILE:(w + 1) * TILE] * factor[first + t, v, b:b + 1, :]
                        total = term if total is None else total + term
                    mixed[b * ROWS:(b + 1) * ROWS, t * TILE:(t + 1) * TILE] = total.astype(BF16)

    def row_product():
        return jnp.dot(row_mat[...], mixed[...], preferred_element_type=F32)

    def far_copy(i, p, s, src, dst):
        return pltpu.make_async_remote_copy(
            src_ref=src, dst_ref=dst, send_sem=far_send.at[i], recv_sem=far_recv.at[i],
            device_id=(p, s), device_id_type=MESH)

    far_same = far_copy(0, after, slab, far_out, far_in)
    far_up = far_copy(1, after, slab - 1, edge_out.at[0], edge_in.at[1])
    far_down = far_copy(2, after, slab + 1, edge_out.at[1], edge_in.at[0])

    def near_copy(i, s, src, dst):
        return pltpu.make_async_remote_copy(
            src_ref=near_out.at[pl.ds(src, NEAR), :], dst_ref=near_in.at[pl.ds(dst, NEAR), :],
            send_sem=near_send.at[i], recv_sem=near_recv.at[i], device_id=(patch, s), device_id_type=MESH)

    near_up = near_copy(0, slab - 1, 0, NEAR)
    near_down = near_copy(1, slab + 1, NEAR, 0)

    def send_to(target):
        if target != 1:
            @pl.when(slab == target)
            def _():
                far_same.start()

        @pl.when(slab == target + 1)
        def _():
            far_up.start()

        @pl.when(slab == target - 1)
        def _():
            far_down.start()

    spread(HALF)
    filtered(HALF, range(NB // 2), True)
    far = row_product()
    far_out[...] = far[EDGE:EDGE + ROWS].astype(BF16)

    links = has_up.astype(jnp.int32) + has_down.astype(jnp.int32)
    pl.semaphore_wait(barrier, 1 + 2 * links)

    @pl.when(slab == 1)
    def _():
        far_same.start()

    def edge(at, rest):
        last = [far[rest:rest + REST, t * TILE:(t + 1) * TILE] for t in range(HALF)]
        return jnp.concatenate([far[at:at + WHOLE], jnp.concatenate(last, axis=0)], axis=1).astype(BF16)

    edge_out[0] = edge(EDGE - WHOLE, EDGE - REACH)
    edge_out[1] = edge(EDGE + ROWS, EDGE + ROWS + WHOLE)
    send_to(1)
    for t in range(HALF - 1):
        tiles[t].wait()
    factors(0)
    spread(0)
    filtered(0, range(0, 4), False)
    send_to(3)
    send_to(2)
    filtered(0, range(4, 10), False)
    send_to(0)
    home = row_product()
    near_out[0:NEAR, :] = home[EDGE - NEAR:EDGE]
    near_out[NEAR:, :] = home[EDGE + ROWS:EDGE + ROWS + NEAR]

    @pl.when(has_up)
    def _():
        near_up.start()

    @pl.when(has_down)
    def _():
        near_down.start()

    other = [visit_scalars(before, v) for v in range(SLOTS)]
    shares = []
    for t in range(HALF):
        weight = jnp.float32(0.0)
        for v in range(SLOTS):
            weight = weight + own[v][0] * own[v][1][t] + other[v][0] * other[v][1][t + HALF]
        shares.append(1.0 / jnp.full((ROWS, TILE), jnp.maximum(weight, 1.0), F32))

    @pl.when(has_up)
    def _():
        near_down.wait_recv()

    @pl.when(has_down)
    def _():
        near_up.wait_recv()

    out[0:NEAR, :] = home[EDGE:EDGE + NEAR] + near_in[0:NEAR, :]
    out[NEAR:ROWS - NEAR, :] = home[EDGE + NEAR:EDGE + ROWS - NEAR]
    out[ROWS - NEAR:, :] = home[EDGE + ROWS - NEAR:EDGE + ROWS] + near_in[NEAR:, :]

    @pl.when(has_up)
    def _():
        far_down.wait_recv()

    @pl.when(has_down)
    def _():
        far_up.wait_recv()

    far_same.wait_recv()
    for t in range(HALF):
        span = slice(t * TILE, (t + 1) * TILE)
        rest = slice(t * REST, (t + 1) * REST)
        ends = edge_in[:, :, span].astype(F32)
        last = edge_in[:, :, WIDE:].astype(F32)
        gap = jnp.zeros((ROWS - 2 * REACH, TILE), F32)
        edges = jnp.concatenate([ends[0], last[0, rest], gap, last[1, rest], ends[1]], axis=0)
        out[:, span] = (out[:, span] + (far_in[:, span].astype(F32) + edges)) * shares[t]

    far_same.wait_send()

    @pl.when(has_up)
    def _():
        far_up.wait_send()
        near_up.wait_send()

    @pl.when(has_down)
    def _():
        far_down.wait_send()
        near_down.wait_send()


def local_part(npatch, nslab, images, row_taps, col_taps, coef, blocks, boxes, ivar, counts):
    vmem = pl.BlockSpec(memory_space=pltpu.VMEM)
    anyplace = pl.BlockSpec(memory_space=pl.ANY)
    dma = pltpu.SemaphoreType.DMA
    return pl.pallas_call(
        functools.partial(kernel, npatch, nslab),
        out_shape=pltpu.VMEM((ROWS, WIDE), F32),
        in_specs=[anyplace] * 8,
        out_specs=vmem,
        scratch_shapes=[
            pltpu.VMEM(row_taps.shape, BF16),
            pltpu.VMEM(col_taps.shape, BF16),
            pltpu.SMEM(boxes.shape[::-1], jnp.int32),
            pltpu.SMEM(ivar.shape, F32),
            pltpu.SMEM(counts.shape, jnp.int32),
            pltpu.VMEM((TILES, SLOTS, ROWS, 2 * TILE), BF16),
            pltpu.VMEM((NB, SETS, TILE), F32),
            pltpu.VMEM((TILES, TILE), jnp.int32),
            pltpu.VMEM((TILE, NB * ROWS), BF16),
            pltpu.VMEM((2 * TILE, NB * TILE), BF16),
            pltpu.VMEM((TILES, SLOTS, 24, TILE), F32),
            pltpu.VMEM((NB * ROWS, WIDE), BF16),
            pltpu.VMEM((ROWS, WIDE), BF16),
            pltpu.VMEM((ROWS, WIDE), BF16),
            pltpu.VMEM((2, WHOLE, WIDE + TILE), BF16),
            pltpu.VMEM((2, WHOLE, WIDE + TILE), BF16),
            pltpu.VMEM((2 * NEAR, WIDE), F32),
            pltpu.VMEM((2 * NEAR, WIDE), F32),
            dma((TILES,)), dma((7,)), dma((3,)), dma((3,)), dma((2,)), dma((2,)),
        ],
        compiler_params=pltpu.CompilerParams(
            collective_id=0, has_side_effects=True, vmem_limit_bytes=56 << 20),
        cost_estimate=pl.CostEstimate(flops=4_000_000_000, bytes_accessed=2_000_000, transcendentals=0),
    )(images, row_taps, col_taps, coef.transpose(2, 1, 0), blocks.T, boxes.T, ivar, counts)


def solution(mesh):
    return jax.shard_map(
        functools.partial(local_part, mesh.shape["ra"], mesh.shape["slab"]),
        mesh=mesh,
        in_specs=(P("ra", "slab", None), P(), P(), P(), P(), P(), P(), P()),
        out_specs=P("slab", "ra"),
        check_vma=False,
    )
```
